32 devices in a mesh: parts: 2 (over x), ep: 16 (over z, y, core), tp: 1.
Axes of the slice: x: 2, y: 2, z: 4, core: 2. Of those that a mesh axis runs over, the one named last changes fastest.
Arguments:
- resid: bfloat16 [512, 3584], P(('parts', 'ep', 'tp')), parts along dimension 0, may hold values from -40 to 40
- norm_gain: float32 [3584], replicated, may hold values from 0.1 to 1.9
- expert_ids: int32 [512, 8], P(('parts', 'ep')), parts along dimension 0, may hold values from 0 to 15, all different within a row; in each aligned block of 16 rows (0 to 15, 16 to 31, ...) at most 16 rows name the same one
- route_weights: bfloat16 [512, 8], P(('parts', 'ep')), parts along dimension 0, may hold values from 0.099609375 to 0.59765625
- gate_up: bfloat16 [16, 3584, 2, 1024], P('ep', None, None, 'tp'), may hold values from -0.09375 to 0.09375
- down: bfloat16 [16, 1024, 3584], P('ep', 'tp'), may hold values from -0.1875 to 0.1875
Outputs:
- layer_out: bfloat16 [512, 3584], P(('parts', 'ep', 'tp')), parts along dimension 0
The draws below stay inside these ranges and needn't reach their ends.
There are 2 independent parts, one for each index of `parts`. The reference program is written for one: setup_inputs(seed, part) draws one part's arguments, and reference() takes and returns one part's arrays. A program takes and returns all parts, laid end to end along the dimension named above; an argument that names none is the same for every part. Nothing has to cross between parts.
Inputs may be any that keep to these rules, and one draw needn't show every extreme that they name: `expert_ids`: each row names 8 different experts. In each aligned block of 16 rows (the rows of one index of ep) no expert is named by more than 16 rows, and in every draw some expert of some block is named by exactly 16 rows.
All inputs are finite; a program needn't handle non-finite values.
Results may differ from the reference program's by a relative error of at most 0.0045.
Values may be sent and summed in bfloat16 or wider, within the bound.
No kernel may reach another device: no remote copies, remote signals or barrier semaphores. Data moves between devices by JAX's collectives and lax.ppermute only.
A program may use at most 128 MiB of HBM per device.

```python
import math
import jax
import jax.numpy as jnp
import numpy as np
from jax import lax

D = 3584
EH = 1024
TOP = 8
REQ_DEV = 16
TOKENS = 256
EXPERTS = 16
CAP = 16
N_EP = 16
N_TP = 1


def draw_resid(key, part):
    key = jax.random.fold_in(key, 7)
    key_base, key_rows, key_cols = jax.random.split(key, 3)
    row_scale = jnp.exp(jax.random.uniform(key_rows, (TOKENS, 1), jnp.float32, math.log(0.3), math.log(3.0)))
    col_scale = jnp.exp(jax.random.uniform(key_cols, (1, D), jnp.float32, math.log(0.3), math.log(3.0)))
    base = jnp.clip(jax.random.normal(key_base, (TOKENS, D), jnp.float32), -4.0, 4.0)
    values = base * row_scale * col_scale
    return jnp.clip(values, -40.0, 40.0).astype(jnp.bfloat16)


def block_levels(key, extent, cuts, low, high):
    loudness, own = 1.0, jax.random.fold_in(key, 6)
    for axis_at, blocks in cuts:
        draws = jnp.exp(jax.random.uniform(jax.random.fold_in(own, axis_at), (blocks,), jnp.float32, low / len(cuts), high / len(cuts)))
        loudness = loudness * jnp.repeat(draws, extent[axis_at] // blocks).reshape([-1 if axis == axis_at else 1 for axis in range(len(extent))])
    return loudness


def shared_out(key, own, number, rows, number_of, top, limit, slope):
    sequence = jax.random.permutation(key, number_of)
    packed, usual = shares(number_of, rows * top, limit, slope, True), shares(number_of, rows * top, limit, slope, False)
    places = jnp.arange(number_of)

    def named(sizes, rotation):
        used = int((sizes > 0).sum())
        fixed = max(1, used // 4)
        shifted = fixed + (places - fixed + rotation * (used - fixed)) % max(1, number_of - fixed)
        return jnp.zeros((number_of,), jnp.int32).at[sequence[jnp.where(places < fixed, places, shifted)]].set(jnp.asarray(sizes, jnp.int32))

    sizes = jnp.where(number % 4 == 0, named(packed, number // 4), named(usual, number - number // 4 - 1))
    mixed = jax.random.permutation(jax.random.fold_in(own, 3), number_of)
    donor, taker = mixed[0:number_of // 2 * 2:2], mixed[1:number_of // 2 * 2:2]
    margin = jnp.minimum(sizes[donor] - 1, limit - sizes[taker]) // 2
    margin = jnp.where((donor == sequence[0]) | (taker == sequence[0]) | (sizes[taker] == 0), 0, jnp.maximum(margin, 0))
    shifted = jax.random.randint(jax.random.fold_in(own, 4), (number_of // 2,), 0, 1 << 20) % (margin + 1)
    sizes = sizes.at[donor].add(-shifted).at[taker].add(shifted)
    labels = jnp.searchsorted(jnp.cumsum(sizes), jnp.arange(rows * top), side="right").astype(jnp.int32)
    listing = labels.reshape(top, rows).T
    listing = listing[jax.random.permutation(jax.random.fold_in(own, 1), rows)]
    rotation = jax.random.randint(jax.random.fold_in(own, 2), (rows, 1), 0, top)
    return jnp.take_along_axis(listing, (jnp.arange(top)[None, :] + rotation) % top, axis=1)


def shares(amount, total, bound, lean, full):
    portions = [(1 << 20) // math.isqrt(standing ** lean) + 1 for standing in range(1, amount + 1)]
    largest = bound if full else min(bound, max(-(-total // amount), total * portions[0] // sum(portions)))
    least = 1 if total - largest >= amount - 1 else 0
    counts, spare = [largest] + [least] * (amount - 1), total - largest - least * (amount - 1)
    while spare > 0:
        free = [i for i in range(1, amount) if counts[i] < largest] or [i for i in range(1, amount) if counts[i] < bound]
        whole, budget = sum([portions[i] for i in free]), spare
        for i in free:
            extra = min(bound - counts[i], max(1, budget * portions[i] // whole), spare)
            counts[i] = counts[i] + extra
            spare = spare - extra
    return np.array(counts)


def centred(stream_key, shape, width, reach, pieces=(), kind=jnp.bfloat16):
    entries = width * jax.random.normal(stream_key, shape, jnp.float32)
    if pieces:
        entries = entries * block_levels(stream_key, shape, pieces, -0.22, 0.18)
    return jnp.clip(entries, -reach, reach).astype(kind)


def setup_inputs(seed: int = 0, part: int = 0) -> dict:
    key_of = jax.random.split(jax.random.key(seed), 7)
    part_splits = jax.random.split(jax.random.fold_in(key_of[6], part), 7)
    resid = draw_resid(jax.random.fold_in(jax.random.fold_in(key_of[6], part), 71), part)
    norm_gain = jnp.clip(1.0 + 0.18 * jax.random.normal(key_of[1], (D,), jnp.float32), 0.1, 1.9)
    expert_ids_keys = jax.random.split(jax.random.fold_in(part_splits[2], 1), TOKENS // (REQ_DEV * N_TP))
    expert_ids_turns = jax.random.permutation(jax.random.fold_in(part_splits[2], 3), TOKENS // (REQ_DEV * N_TP))
    expert_ids = jax.vmap(lambda own, number: shared_out(jax.random.fold_in(part_splits[2], 2), own, number, REQ_DEV * N_TP, EXPERTS, TOP, CAP, 2))(expert_ids_keys, expert_ids_turns).reshape((TOKENS, TOP))
    route_weights = jnp.clip(jnp.exp(math.log(0.59765625) - 1.7917595 * jax.random.uniform(part_splits[3], (TOKENS, TOP), jnp.float32) ** block_levels(part_splits[3], (TOKENS, TOP), ((0, 16),), -0.2, 0.2)), 0.099609375, 0.59765625).astype(jnp.bfloat16)
    gate_up = centred(key_of[4], (EXPERTS, D, 2, EH), D ** -0.5, 0.09375, ((0, 16),))
    down = centred(key_of[5], (EXPERTS, EH, D), EH ** -0.5, 0.1875, ((0, 16),))
    return {"resid": resid, "norm_gain": norm_gain, "expert_ids": expert_ids, "route_weights": route_weights, "gate_up": gate_up, "down": down}


def reference(resid, norm_gain, expert_ids, route_weights, gate_up, down):
    values = resid.astype(jnp.float32)
    scale = lax.rsqrt(lax.optimization_barrier(jnp.mean(values * values, axis=-1, keepdims=True)) + 1e-06)
    normed = (values * scale * norm_gain).astype(jnp.bfloat16)
    rows_cap = min(N_EP * CAP, TOKENS)
    block = EH // N_TP

    def step(total, expert):
        hit = expert_ids == expert
        share = lax.optimization_barrier(jnp.sum(jnp.where(hit, route_weights.astype(jnp.float32), 0.0), axis=1))
        named = jnp.any(hit, axis=1).astype(jnp.int32)
        order = jnp.argsort(1 - named, stable=True)[:rows_cap].astype(jnp.int32)
        rows = normed[order]
        weights_gu = gate_up[expert].reshape(D, 2 * EH)
        both = jnp.dot(rows, weights_gu, preferred_element_type=jnp.float32)
        hidden = (jax.nn.silu(both[:, :EH]) * both[:, EH:]).astype(jnp.bfloat16)
        weights_down = down[expert]
        output = jnp.zeros((rows_cap, D), jnp.float32)
        for index in range(N_TP):
            piece = jnp.dot(hidden[:, index * block:(index + 1) * block], weights_down[index * block:(index + 1) * block], preferred_element_type=jnp.float32).astype(jnp.bfloat16)
            piece = lax.optimization_barrier(piece)
            output = output + piece.astype(jnp.float32)
        contrib = share[order][:, None] * output
        return (total.at[order].add(contrib), None)
    total = jnp.zeros((TOKENS, D), jnp.float32)
    total, _ = lax.scan(step, total, jnp.arange(EXPERTS, dtype=jnp.int32))
    return (values + total).astype(jnp.bfloat16)
```

```python
import jax
import jax.numpy as jnp
from jax import lax
from jax.sharding import PartitionSpec as P

eps = 1e-06


def swap(block, offset):
    count = lax.axis_size("ep")
    return lax.ppermute(block, "ep", [(i, i ^ offset) for i in range(count)])


def gather_blocks(block, far):
    near = {0: block}
    for offset in far:
        near[offset] = swap(block, offset)
    for offset in (0, *far):
        source = block if offset == far[0] else near[offset]
        near[offset ^ 2] = swap(source, offset ^ 2 if offset == far[0] else 2)
    for offset in list(near):
        near[offset ^ 1] = swap(near[offset], 1)
    return near


def shards(resid, norm_gain, expert_ids, route_weights, gate_up, down):
    values = resid.astype(jnp.float32)
    width = resid.shape[1]
    owners = lax.axis_size("ep")
    owner = lax.axis_index("ep")
    far = tuple(range(4, owners, 4))
    scale = lax.rsqrt(jnp.mean(values * values, axis=-1, keepdims=True) + eps)
    normed = (values * scale * norm_gain).astype(jnp.bfloat16)
    normed = lax.all_gather(normed, "tp", axis=0, tiled=True)
    rows = normed.shape[0]
    lanes = jnp.arange(128, dtype=jnp.int32)
    share_all = jnp.sum(
        jnp.where(expert_ids[:, :, None] == lanes, route_weights[:, :, None], 0), axis=1
    ).astype(jnp.bfloat16)
    blocks = gather_blocks(jnp.concatenate([normed, share_all], axis=1), far)
    order = sorted(blocks, key=lambda o: (1 - (o & 1), 1 - (o >> 1 & 1), -o))
    everything = jnp.concatenate([blocks[o] for o in order], axis=0)
    share = jnp.sum(
        jnp.where(lanes == owner, everything[:, width:].astype(jnp.float32), 0.0),
        axis=1,
        keepdims=True,
    )
    weights_gu = gate_up[0].reshape(width, -1)
    inner = down.shape[1]
    both = jnp.dot(everything[:, :width], weights_gu, preferred_element_type=jnp.float32)
    hidden = (jax.nn.silu(both[:, :inner]) * both[:, inner:]).astype(jnp.bfloat16)
    piece = jnp.dot(hidden, down[0], preferred_element_type=jnp.float32).astype(jnp.bfloat16)
    terms = (share * piece.astype(jnp.float32)).astype(jnp.bfloat16)
    place = {o: at for at, o in enumerate(order)}
    half = owners // 2 * rows
    quarter = half // 2
    add = lambda a, b: a.astype(jnp.float32) + b.astype(jnp.float32)
    total = add(swap(terms[:half], 1), terms[half:]).astype(jnp.bfloat16)
    parts = {}
    for at, offset in enumerate(o for o in order if o & 3 == 0):
        away = total[at * rows : (at + 1) * rows]
        here = total[quarter + at * rows : quarter + (at + 1) * rows]
        parts[offset] = add(swap(away, 2), here)
    mine = parts[0]
    for offset in reversed(far):
        mine = mine + swap(parts[offset].astype(jnp.bfloat16), offset).astype(jnp.float32)
    mine = lax.psum_scatter(mine, "tp", scatter_dimension=0, tiled=True)
    return (values + mine).astype(jnp.bfloat16)


def solution(mesh):
    return jax.shard_map(
        shards,
        mesh=mesh,
        in_specs=(
            P(("parts", "ep", "tp"), None),
            P(),
            P(("parts", "ep"), None),
            P(("parts", "ep"), None),
            P("ep", None, None, "tp"),
            P("ep", "tp", None),
        ),
        out_specs=P(("parts", "ep", "tp"), None),
        check_vma=False,
    )
```

```python
import functools

import jax
import jax.numpy as jnp
from jax import lax
from jax.experimental import pallas as pl
from jax.experimental.pallas import tpu as pltpu
from jax.sharding import PartitionSpec as P

eps = 1e-06
lane = 128
VMEM = pl.BlockSpec(memory_space=pltpu.VMEM)
ANY = pl.BlockSpec(memory_space=pl.ANY)
HBM = pl.BlockSpec(memory_space=pltpu.HBM)


def limit(mib):
    return pltpu.CompilerParams(vmem_limit_bytes=mib << 20)


def in_hbm(array):
    return pltpu.with_memory_space_constraint(array, pltpu.HBM)


def in_vmem(array):
    return pltpu.with_memory_space_constraint(array, pltpu.VMEM)


def norm_kernel(*refs):
    sources, out_ref, held, sems = refs[:4], refs[4], refs[5:9], refs[9]
    copies = [
        pltpu.make_async_copy(source, ref, sems.at[i])
        for i, (source, ref) in enumerate(zip(sources, held))
    ]
    for copy in copies:
        copy.start()
    for copy in copies:
        copy.wait()
    resid_ref, gain_ref, ids_ref, weights_ref = held
    rows, width = resid_ref.shape
    values = resid_ref[...].astype(jnp.float32)
    scale = lax.rsqrt(jnp.mean(values * values, axis=-1, keepdims=True) + eps)
    gain = gain_ref[...].reshape(1, width)
    out_ref[:, :width] = (values * scale * gain).astype(jnp.bfloat16)
    chosen, count = ids_ref.shape
    experts = lax.broadcasted_iota(jnp.int32, (lane, count), 0)
    share = jnp.zeros((lane, count), jnp.float32)
    for k in range(chosen):
        weight = weights_ref[k : k + 1, :].astype(jnp.float32)
        share = share + jnp.where(experts == ids_ref[k : k + 1, :], weight, 0.0)
    out_ref[:, width:] = share.T.astype(jnp.bfloat16)


def norm(resid, gain, ids, weights):
    rows, width = resid.shape
    sources = [resid, gain, ids.T, weights.T]
    return pl.pallas_call(
        norm_kernel,
        out_shape=jax.ShapeDtypeStruct((rows, width + lane), jnp.bfloat16),
        in_specs=[HBM] * 4,
        out_specs=VMEM,
        scratch_shapes=[pltpu.VMEM(a.shape, a.dtype) for a in sources]
        + [pltpu.SemaphoreType.DMA((4,))],
        compiler_params=limit(3),
        name="norm",
    )(*[in_hbm(a) for a in sources])


def unpack_kernel(first, packed_ref, *refs):
    out_ref, token_ref, buffer, sems = refs[-4:]
    token_ref[...] = jnp.zeros_like(token_ref)
    width = packed_ref.shape[1]
    groups = buffer.shape[0]
    inner = groups * lane
    copies = [
        pltpu.make_async_copy(
            packed_ref.at[0, :, :, (first + c) * lane : (first + c + 1) * lane],
            buffer.at[c],
            sems.at[c],
        )
        for c in range(groups)
    ]
    for copy in copies:
        copy.start()
    tile = 128
    for c in range(groups):
        copies[c].wait()
        rows = buffer.at[c].reshape(2 * width, lane)

        def step(i, _):
            both = rows.at[pl.ds(pl.multiple_of(i * 2 * tile, 2 * tile), 2 * tile), :]
            to = pl.ds(pl.multiple_of(i * tile, tile), tile)
            out_ref[to, c * lane : (c + 1) * lane] = both[pl.ds(0, tile, stride=2), :]
            out_ref[to, inner + c * lane : inner + (c + 1) * lane] = both[
                pl.ds(1, tile, stride=2), :
            ]
            return 0

        lax.fori_loop(0, width // tile, step, 0, unroll=2)


def unpack(packed, first, groups, after):
    width = packed.shape[1]
    return pl.pallas_call(
        functools.partial(unpack_kernel, first),
        out_shape=[
            jax.ShapeDtypeStruct((width, 2 * groups * lane), jnp.bfloat16),
            jax.ShapeDtypeStruct((8, lane), jnp.float32),
        ],
        in_specs=[HBM] + [ANY] * len(after),
        out_specs=[VMEM, VMEM],
        scratch_shapes=[
            pltpu.VMEM((groups, width, 2, lane), jnp.bfloat16),
            pltpu.SemaphoreType.DMA((groups,)),
        ],
        compiler_params=limit(9),
        cost_estimate=pl.CostEstimate(
            flops=0, bytes_accessed=8 * width * groups * lane, transcendentals=0
        ),
        name="unpack",
    )(in_hbm(packed), *after)


def pass_kernel(*refs):
    count = (len(refs) - 1) // 2
    for source, out_ref in zip(refs[:count], refs[count + 1 :]):
        out_ref[...] = source[...]


def pass_on(blocks, after):
    return pl.pallas_call(
        pass_kernel,
        out_shape=[jax.ShapeDtypeStruct(b.shape, b.dtype) for b in blocks],
        in_specs=[VMEM] * len(blocks) + [ANY],
        out_specs=[VMEM] * len(blocks),
        compiler_params=limit(2),
        name="pass_on",
    )(*blocks, after)


def hidden_rows(rows_ref, gu_refs, hidden, at, tile):
    step = 256
    to = 0
    rows = rows_ref[at : at + tile, : gu_refs[0].shape[0]]
    for gu_ref in gu_refs:
        half = gu_ref.shape[1] // 2
        for n in range(0, half, step):
            gate = jnp.dot(rows, gu_ref[:, n : n + step], preferred_element_type=jnp.float32)
            up = jnp.dot(
                rows, gu_ref[:, half + n : half + n + step], preferred_element_type=jnp.float32
            )
            hidden[at : at + tile, to : to + step] = (jax.nn.silu(gate) * up).astype(jnp.bfloat16)
            to += step


def near_kernel(count, *refs):
    block_refs, gu_refs = refs[:count], refs[count:-2]
    hidden, rows_ref = refs[-2:]
    size = block_refs[0].shape[0]
    for at, block_ref in enumerate(block_refs):
        rows_ref[at * size : (at + 1) * size, :] = block_ref[...]
    tile = min(256, size * count)
    for at in range(0, size * count, tile):
        hidden_rows(rows_ref, gu_refs, hidden, at, tile)


def near_hidden(blocks, halves):
    size, wide = blocks[0].shape
    count = size * len(blocks)
    width, inner = halves[0].shape[0], sum(h.shape[1] // 2 for h in halves)
    return pl.pallas_call(
        functools.partial(near_kernel, len(blocks)),
        out_shape=jax.ShapeDtypeStruct((count, inner), jnp.bfloat16),
        in_specs=[VMEM] * (len(blocks) + len(halves)),
        out_specs=VMEM,
        scratch_shapes=[pltpu.VMEM((count, wide), jnp.bfloat16)],
        compiler_params=limit(6),
        cost_estimate=pl.CostEstimate(
            flops=4 * count * width * inner, bytes_accessed=0, transcendentals=count * inner
        ),
        name="near",
    )(*blocks, *halves)


def expert_kernel(near_count, far_count, order, down_hbm, near_hidden_ref, *refs):
    near_refs, far_refs = refs[:near_count], refs[near_count : near_count + far_count]
    gu_refs = refs[near_count + far_count : -7]
    away_ref, here_ref, rows_ref, far_hidden, hidden, down_ref, sem = refs[-7:]
    copy = pltpu.make_async_copy(down_hbm, down_ref, sem)
    copy.start()
    inner, width = down_ref.shape[1:]
    count = hidden.shape[0]
    size = near_refs[0].shape[0]
    for at, block_ref in enumerate(far_refs):
        rows_ref[at * size : (at + 1) * size, :] = block_ref[...]
    tile = min(256, size * far_count)
    for at in range(0, size * far_count, tile):
        hidden_rows(rows_ref, gu_refs, far_hidden, at, tile)
    shares = []
    for to, (near, at) in enumerate(order):
        source = near_hidden_ref if near else far_hidden
        hidden[to * size : (to + 1) * size, :] = source[at * size : (at + 1) * size, :]
        shares.append((near_refs if near else far_refs)[at][:, width:].astype(jnp.float32))
    shares = jnp.concatenate(shares, axis=0)
    lanes = lax.broadcasted_iota(jnp.int32, shares.shape, 1)
    share = jnp.sum(jnp.where(lanes == lax.axis_index("ep"), shares, 0.0), axis=1, keepdims=True)
    copy.wait()
    half = count // 2
    tile = min(256, count)
    step = 512
    for at in range(0, count, tile):
        for n in range(0, width, step):
            piece = jnp.dot(
                hidden[at : at + tile, :],
                down_ref[0, :, n : n + step],
                preferred_element_type=jnp.float32,
            )
            piece = piece.astype(jnp.bfloat16).astype(jnp.float32)
            terms = (share[at : at + tile] * piece).astype(jnp.bfloat16)
            if tile > half:
                away_ref[:, n : n + step] = terms[:half]
                here_ref[:, n : n + step] = terms[half:]
            else:
                out_ref, to = (away_ref, at) if at < half else (here_ref, at - half)
                out_ref[to : to + tile, n : n + step] = terms


def expert(down, near, far, halves, order):
    hidden = near_hidden(near, halves)
    size = near[0].shape[0]
    count = size * (len(near) + len(far))
    _, inner, width = down.shape
    return pl.pallas_call(
        functools.partial(expert_kernel, len(near), len(far), order),
        out_shape=[jax.ShapeDtypeStruct((count // 2, width), jnp.bfloat16)] * 2,
        in_specs=[HBM] + [VMEM] * (1 + len(near) + len(far) + len(halves)),
        out_specs=[VMEM, VMEM],
        scratch_shapes=[
            pltpu.VMEM((size * len(far), width + lane), jnp.bfloat16),
            pltpu.VMEM((size * len(far), inner), jnp.bfloat16),
            pltpu.VMEM((count, inner), jnp.bfloat16),
            pltpu.VMEM(down.shape, jnp.bfloat16),
            pltpu.SemaphoreType.DMA,
        ],
        compiler_params=limit(16 if count <= 256 else 43),
        cost_estimate=pl.CostEstimate(
            flops=4 * count * width * inner,
            bytes_accessed=2 * width * inner,
            transcendentals=count * inner // 2,
        ),
        name="expert",
    )(in_hbm(down), hidden, *near, *far, *halves)


def fold_kernel(got_ref, here_ref, *out_refs):
    *away_refs, rest_ref = out_refs
    rows = away_refs[0].shape[0]
    for at, away_ref in enumerate(away_refs):
        part = slice(at * rows, (at + 1) * rows)
        total = got_ref[part, :].astype(jnp.float32) + here_ref[part, :].astype(jnp.float32)
        away_ref[...] = total.astype(jnp.bfloat16)
    rest = rest_ref.shape[0]
    at = got_ref.shape[0] - rest
    total = got_ref[at:, :].astype(jnp.float32) + here_ref[at:, :].astype(jnp.float32)
    rest_ref[...] = total.astype(jnp.bfloat16)


def fold(got, here, count):
    total, width = got.shape
    shape = jax.ShapeDtypeStruct
    return pl.pallas_call(
        fold_kernel,
        out_shape=[shape((total // 2 // count, width), jnp.bfloat16)] * count
        + [shape((total // 2, width), jnp.bfloat16)],
        in_specs=[VMEM, VMEM],
        out_specs=[VMEM] * (count + 1),
        compiler_params=pltpu.CompilerParams(vmem_limit_bytes=6 << 20),
        name="fold",
    )(got, here)


def add_kernel(at, got_ref, here_ref, out_ref):
    rows = got_ref.shape[0]
    here = here_ref[at : at + rows, :].astype(jnp.float32)
    out_ref[...] = (got_ref[...].astype(jnp.float32) + here).astype(jnp.bfloat16)


def add(got, here, at):
    return pl.pallas_call(
        functools.partial(add_kernel, at),
        out_shape=jax.ShapeDtypeStruct(got.shape, jnp.bfloat16),
        in_specs=[VMEM, VMEM],
        out_specs=VMEM,
        compiler_params=pltpu.CompilerParams(vmem_limit_bytes=2 << 20),
        name="add",
    )(got, here)


def swap(block, offset):
    count = lax.axis_size("ep")
    return lax.ppermute(block, "ep", [(i, i ^ offset) for i in range(count)])


def gather_blocks(block, far, weights):
    near = {0: block}
    for offset in reversed(far):
        near[offset] = swap(block, offset)
    first, token = weights(0, [])
    (again,) = pass_on([block], token)
    for offset in (2, far[0] ^ 2):
        near[offset] = swap(again, offset)
    near[1] = swap(again, 1)
    late = far[:0:-1]
    second, _ = weights(1, [near[late[0]]])
    for offset in late:
        near[offset ^ 2] = swap(near[offset], 2)
    for offset in list(near):
        if offset > 1:
            near[offset ^ 1] = swap(near[offset], 1)
    return near, [first, second]


def shards(resid, norm_gain, expert_ids, route_weights, gate_up, down):
    owners = lax.axis_size("ep")
    tp = lax.axis_size("tp")
    far = tuple(range(4, owners, 4))
    inner = down.shape[1]
    resid_all = lax.all_gather(resid, "tp", axis=0, tiled=True) if tp > 1 else resid
    normed = norm(resid_all, norm_gain, expert_ids, route_weights)
    rows = normed.shape[0]
    groups = inner // lane
    cuts = ((0, groups // 2), (groups // 2, groups - groups // 2))
    blocks, halves = gather_blocks(
        normed, far, lambda i, after: unpack(gate_up, *cuts[i], after)
    )
    order = sorted(blocks, key=lambda o: (1 - (o & 1), 1 - (o >> 1 & 1), -o))
    places = [(o < 8, o % 8 if o < 8 else o - 8) for o in order]
    near = [blocks[o] for o in range(8)]
    away, here = expert(
        down, near, [blocks[o] for o in range(8, owners)], halves, places
    )
    *away, here = fold(swap(away, 1), here, len(far) + 1)
    evens = [o for o in order if o & 3 == 0]
    got = {offset: swap(block, 2) for offset, block in zip(evens, away)}
    mine = None
    for at, offset in enumerate(evens):
        if offset:
            part = swap(add(got[offset], here, at * rows), offset).astype(jnp.float32)
        else:
            part = got[0].astype(jnp.float32) + here[at * rows :].astype(jnp.float32)
        mine = part if mine is None else mine + part
    if tp > 1:
        mine = lax.psum_scatter(mine, "tp", scatter_dimension=0, tiled=True)
    return (resid.astype(jnp.float32) + mine).astype(jnp.bfloat16)


def solution(mesh):
    return jax.shard_map(
        shards,
        mesh=mesh,
        in_specs=(
            P(("parts", "ep", "tp"), None),
            P(),
            P(("parts", "ep"), None),
            P(("parts", "ep"), None),
            P("ep", None, None, "tp"),
            P("ep", "tp", None),
        ),
        out_specs=P(("parts", "ep", "tp"), None),
        check_vma=False,
    )
```

```python
import functools

import jax
import jax.numpy as jnp
from jax import lax
from jax.experimental import pallas as pl
from jax.experimental.pallas import tpu as pltpu
from jax.sharding import PartitionSpec as P

eps = 1e-06
lane = 128
VMEM = pl.BlockSpec(memory_space=pltpu.VMEM)
ANY = pl.BlockSpec(memory_space=pl.ANY)
HBM = pl.BlockSpec(memory_space=pltpu.HBM)


def limit(mib):
    return pltpu.CompilerParams(vmem_limit_bytes=mib << 20)


def in_hbm(array):
    return pltpu.with_memory_space_constraint(array, pltpu.HBM)


def in_vmem(array):
    return pltpu.with_memory_space_constraint(array, pltpu.VMEM)


def norm_kernel(*refs):
    sources, out_ref, held, sems = refs[:4], refs[4], refs[5:9], refs[9]
    copies = [
        pltpu.make_async_copy(source, ref, sems.at[i])
        for i, (source, ref) in enumerate(zip(sources, held))
    ]
    for copy in copies:
        copy.start()
    for copy in copies:
        copy.wait()
    resid_ref, gain_ref, ids_ref, weights_ref = held
    rows, width = resid_ref.shape
    values = resid_ref[...].astype(jnp.float32)
    scale = lax.rsqrt(jnp.mean(values * values, axis=-1, keepdims=True) + eps)
    gain = gain_ref[...].reshape(1, width)
    out_ref[:, :width] = (values * scale * gain).astype(jnp.bfloat16)
    chosen, count = ids_ref.shape
    experts = lax.broadcasted_iota(jnp.int32, (lane, count), 0)
    share = jnp.zeros((lane, count), jnp.float32)
    for k in range(chosen):
        weight = weights_ref[k : k + 1, :].astype(jnp.float32)
        share = share + jnp.where(experts == ids_ref[k : k + 1, :], weight, 0.0)
    out_ref[:, width:] = share.T.astype(jnp.bfloat16)


def norm(resid, gain, ids, weights):
    rows, width = resid.shape
    sources = [resid, gain, ids.T, weights.T]
    return pl.pallas_call(
        norm_kernel,
        out_shape=jax.ShapeDtypeStruct((rows, width + lane), jnp.bfloat16),
        in_specs=[HBM] * 4,
        out_specs=VMEM,
        scratch_shapes=[pltpu.VMEM(a.shape, a.dtype) for a in sources]
        + [pltpu.SemaphoreType.DMA((4,))],
        compiler_params=limit(3),
        name="norm",
    )(*[in_hbm(a) for a in sources])


def unpack_kernel(first, packed_ref, *refs):
    out_ref, token_ref, buffer, sems = refs[-4:]
    token_ref[...] = jnp.zeros_like(token_ref)
    width = packed_ref.shape[1]
    groups = buffer.shape[0]
    inner = groups * lane
    copies = [
        pltpu.make_async_copy(
            packed_ref.at[0, :, :, (first + c) * lane : (first + c + 1) * lane],
            buffer.at[c],
            sems.at[c],
        )
        for c in range(groups)
    ]
    for copy in copies:
        copy.start()
    tile = 128
    for c in range(groups):
        copies[c].wait()
        rows = buffer.at[c].reshape(2 * width, lane)

        def step(i, _):
            both = rows.at[pl.ds(pl.multiple_of(i * 2 * tile, 2 * tile), 2 * tile), :]
            to = pl.ds(pl.multiple_of(i * tile, tile), tile)
            out_ref[to, c * lane : (c + 1) * lane] = both[pl.ds(0, tile, stride=2), :]
            out_ref[to, inner + c * lane : inner + (c + 1) * lane] = both[
                pl.ds(1, tile, stride=2), :
            ]
            return 0

        lax.fori_loop(0, width // tile, step, 0, unroll=2)


def unpack(packed, first, groups, after, cost=0):
    width = packed.shape[1]
    return pl.pallas_call(
        functools.partial(unpack_kernel, first),
        out_shape=[
            jax.ShapeDtypeStruct((width, 2 * groups * lane), jnp.bfloat16),
            jax.ShapeDtypeStruct((8, lane), jnp.float32),
        ],
        in_specs=[HBM] + [ANY] * len(after),
        out_specs=[VMEM, VMEM],
        scratch_shapes=[
            pltpu.VMEM((groups, width, 2, lane), jnp.bfloat16),
            pltpu.SemaphoreType.DMA((groups,)),
        ],
        compiler_params=limit(9),
        cost_estimate=pl.CostEstimate(flops=0, bytes_accessed=cost, transcendentals=0),
        name="unpack",
    )(in_hbm(packed), *after)


def pass_kernel(*refs):
    count = (len(refs) - 1) // 2
    for source, out_ref in zip(refs[:count], refs[count + 1 :]):
        out_ref[...] = source[...]


def pass_on(blocks, after):
    return pl.pallas_call(
        pass_kernel,
        out_shape=[jax.ShapeDtypeStruct(b.shape, b.dtype) for b in blocks],
        in_specs=[VMEM] * len(blocks) + [ANY],
        out_specs=[VMEM] * len(blocks),
        compiler_params=limit(2),
        name="pass_on",
    )(*blocks, after)


def hidden_rows(rows_ref, gu_refs, hidden, at, tile):
    to = 0
    rows = rows_ref[at : at + tile, : gu_refs[0].shape[0]]
    for gu_ref in gu_refs:
        half = gu_ref.shape[1] // 2
        step = min(256, half)
        for n in range(0, half, step):
            gate = jnp.dot(rows, gu_ref[:, n : n + step], preferred_element_type=jnp.float32)
            up = jnp.dot(
                rows, gu_ref[:, half + n : half + n + step], preferred_element_type=jnp.float32
            )
            hidden[at : at + tile, to : to + step] = (jax.nn.silu(gate) * up).astype(jnp.bfloat16)
            to += step


def near_kernel(count, after, *refs):
    block_refs, gu_refs = refs[:count], refs[count : -2 - after]
    hidden, rows_ref = refs[-2:]
    size = block_refs[0].shape[0]
    for at, block_ref in enumerate(block_refs):
        rows_ref[at * size : (at + 1) * size, :] = block_ref[...]
    tile = min(256, size * count)
    for at in range(0, size * count, tile):
        hidden_rows(rows_ref, gu_refs, hidden, at, tile)


def near_hidden(blocks, halves, after):
    size, wide = blocks[0].shape
    count = size * len(blocks)
    width, inner = halves[0].shape[0], sum(h.shape[1] // 2 for h in halves)
    return pl.pallas_call(
        functools.partial(near_kernel, len(blocks), len(after)),
        out_shape=jax.ShapeDtypeStruct((count, inner), jnp.bfloat16),
        in_specs=[VMEM] * (len(blocks) + len(halves)) + [ANY] * len(after),
        out_specs=VMEM,
        scratch_shapes=[pltpu.VMEM((count, wide), jnp.bfloat16)],
        compiler_params=limit(6),
        cost_estimate=pl.CostEstimate(flops=0, bytes_accessed=0, transcendentals=0),
        name="near",
    )(*blocks, *halves, *after)


def down_rows(hidden, share, down_ref, out_ref):
    count, width = out_ref.shape
    tile = min(256, count)
    step = 512
    for at in range(0, count, tile):
        for n in range(0, width, step):
            piece = jnp.dot(
                hidden[at : at + tile, :],
                down_ref[0, :, n : n + step],
                preferred_element_type=jnp.float32,
            )
            piece = piece.astype(jnp.bfloat16).astype(jnp.float32)
            terms = (share[at : at + tile, :1] * piece).astype(jnp.bfloat16)
            out_ref[at : at + tile, n : n + step] = terms


def away_kernel(near_count, far_count, order, down_ref, near_hidden_ref, *refs):
    near_refs, far_refs = refs[:near_count], refs[near_count : near_count + far_count]
    gu_refs = refs[near_count + far_count : -6]
    away_ref, here_hidden, here_share, rows_ref, far_hidden, away_hidden = refs[-6:]
    width = down_ref.shape[2]
    size = near_refs[0].shape[0]
    for at, block_ref in enumerate(far_refs):
        rows_ref[at * size : (at + 1) * size, :] = block_ref[...]
    tile = min(256, size * far_count)
    for at in range(0, size * far_count, tile):
        hidden_rows(rows_ref, gu_refs, far_hidden, at, tile)
    half = len(order) // 2
    lanes = lax.broadcasted_iota(jnp.int32, (size, lane), 1)
    parts = []
    for to, (near, at) in enumerate(order):
        source = near_hidden_ref if near else far_hidden
        block = (near_refs if near else far_refs)[at][:, width:].astype(jnp.float32)
        mine = jnp.where(lanes == lax.axis_index("ep"), block, 0.0)
        share = jnp.sum(mine, axis=1, keepdims=True)
        place = slice(to % half * size, (to % half + 1) * size)
        if to < half:
            away_hidden[place, :] = source[at * size : (at + 1) * size, :]
            parts.append(share)
        else:
            here_hidden[place, :] = source[at * size : (at + 1) * size, :]
            here_share[place, :] = jnp.broadcast_to(share, (size, lane))
    down_rows(away_hidden, jnp.concatenate(parts, axis=0), down_ref, away_ref)


def here_kernel(down_ref, hidden_ref, share_ref, out_ref):
    down_rows(hidden_ref, share_ref, down_ref, out_ref)


def expert(down, hidden, near, far, halves, order):
    size = near[0].shape[0]
    count = size * (len(near) + len(far))
    half = count // 2
    _, inner, width = down.shape
    shape = jax.ShapeDtypeStruct
    away, here_hidden, here_share = pl.pallas_call(
        functools.partial(away_kernel, len(near), len(far), order),
        out_shape=[
            shape((half, width), jnp.bfloat16),
            shape((half, inner), jnp.bfloat16),
            shape((half, lane), jnp.float32),
        ],
        in_specs=[VMEM] * (2 + len(near) + len(far) + len(halves)),
        out_specs=[VMEM] * 3,
        scratch_shapes=[
            pltpu.VMEM((size * len(far), width + lane), jnp.bfloat16),
            pltpu.VMEM((size * len(far), inner), jnp.bfloat16),
            pltpu.VMEM((half, inner), jnp.bfloat16),
        ],
        compiler_params=limit(8 if count <= 256 else 24),
        cost_estimate=pl.CostEstimate(
            flops=3 * count * width * inner, bytes_accessed=0, transcendentals=count * inner // 2
        ),
        name="away",
    )(down, hidden, *near, *far, *halves)
    here = pl.pallas_call(
        here_kernel,
        out_shape=shape((half, width), jnp.bfloat16),
        in_specs=[VMEM] * 3,
        out_specs=VMEM,
        compiler_params=limit(4 if count <= 256 else 8),
        cost_estimate=pl.CostEstimate(
            flops=count * width * inner, bytes_accessed=0, transcendentals=0
        ),
        name="here",
    )(down, here_hidden, here_share)
    return away, here


def fold_kernel(got_ref, here_ref, *out_refs):
    *away_refs, rest_ref = out_refs
    rows = away_refs[0].shape[0]
    for at, away_ref in enumerate(away_refs):
        part = slice(at * rows, (at + 1) * rows)
        total = got_ref[part, :].astype(jnp.float32) + here_ref[part, :].astype(jnp.float32)
        away_ref[...] = total.astype(jnp.bfloat16)
    rest = rest_ref.shape[0]
    at = got_ref.shape[0] - rest
    total = got_ref[at:, :].astype(jnp.float32) + here_ref[at:, :].astype(jnp.float32)
    rest_ref[...] = total.astype(jnp.bfloat16)


def fold(got, here, count):
    total, width = got.shape
    shape = jax.ShapeDtypeStruct
    return pl.pallas_call(
        fold_kernel,
        out_shape=[shape((total // 2 // count, width), jnp.bfloat16)] * count
        + [shape((total // 2, width), jnp.bfloat16)],
        in_specs=[VMEM, VMEM],
        out_specs=[VMEM] * (count + 1),
        compiler_params=pltpu.CompilerParams(vmem_limit_bytes=6 << 20),
        name="fold",
    )(got, here)


def add_kernel(at, got_ref, here_ref, *refs):
    count = (len(refs) - 1) // 2
    out_ref = refs[count]
    rows = got_ref.shape[0]
    here = here_ref[at : at + rows, :].astype(jnp.float32)
    out_ref[...] = (got_ref[...].astype(jnp.float32) + here).astype(jnp.bfloat16)
    for source, copy_ref in zip(refs[:count], refs[count + 1 :]):
        copy_ref[...] = source[...]


def add(got, here, at, *later):
    return pl.pallas_call(
        functools.partial(add_kernel, at),
        out_shape=[jax.ShapeDtypeStruct(got.shape, jnp.bfloat16)] * (1 + len(later)),
        in_specs=[VMEM] * (2 + len(later)),
        out_specs=[VMEM] * (1 + len(later)),
        compiler_params=limit(2),
        name="add",
    )(got, here, *later)


def swap(block, offset):
    count = lax.axis_size("ep")
    return lax.ppermute(block, "ep", [(i, i ^ offset) for i in range(count)])


def gather_blocks(block, far, gate_up):
    groups = gate_up.shape[3] // lane // 2
    near = {0: block}
    lead, *late = far[:0:-1]
    close = far[0]
    near[lead], near[2] = swap(block, lead), swap(block, 2)
    first, token = unpack(gate_up, 0, groups, [], 1 << 24)
    (again,) = pass_on([block], token)
    for offset in (*late, close, close ^ 2):
        near[offset] = swap(again, offset)
    (near[lead],) = pass_on([near[lead]], near[2])
    near[lead ^ 2] = swap(near[lead], 2)
    second, token = unpack(gate_up, groups, gate_up.shape[3] // lane - groups, [again], 1 << 24)
    first_late = (lead, lead ^ 2, *late)
    near[lead], near[lead ^ 2], *held = pass_on([near[offset] for offset in first_late], token)
    for offset, array in zip(late, held):
        near[offset] = array
        near[offset ^ 2] = swap(array, 2)
    ready = (0, 2, close, close ^ 2)
    near[lead ^ 1] = swap(near[lead], 1)
    for offset, array in zip(ready, pass_on([near[offset] for offset in ready], near[lead ^ 1])):
        near[offset] = array
    for offset in (*ready, lead ^ 2, *late):
        near[offset ^ 1] = swap(near[offset], 1)
    for offset in late:
        near[offset ^ 3] = swap(near[offset ^ 2], 1)
    hidden = near_hidden(
        [near[offset] for offset in range(8)], [first, second], [near[late[-1] ^ 2]]
    )
    return near, [first, second], hidden


def shards(resid, norm_gain, expert_ids, route_weights, gate_up, down):
    owners = lax.axis_size("ep")
    tp = lax.axis_size("tp")
    far = tuple(range(4, owners, 4))
    resid_all = lax.all_gather(resid, "tp", axis=0, tiled=True) if tp > 1 else resid
    normed = norm(resid_all, norm_gain, expert_ids, route_weights)
    rows = normed.shape[0]
    blocks, parts, hidden = gather_blocks(normed, far, gate_up)
    order = sorted(blocks, key=lambda o: (1 - (o & 1), 1 - (o >> 1 & 1), -o))
    places = [(o < 8, o % 8 if o < 8 else o - 8) for o in order]
    near, late = [blocks[o] for o in range(8)], [blocks[o] for o in range(8, owners)]
    away, here = expert(down, hidden, near, late, parts, places)
    *away, here = fold(swap(away, 1), here, len(far) + 1)
    away = dict(zip((o for o in order if o & 3 == 0), away))
    at_rows = {o: at * rows for at, o in enumerate(away)}
    close, late = far[0], far[:0:-1]
    got = {offset: swap(away[offset], 2) for offset in late}
    beside = swap(here[at_rows[close] : at_rows[close] + rows], close)
    later = [away[close], away[0], beside]
    sent = []
    for offset in late:
        if offset == late[-1]:
            block, *later = add(got[offset], here, at_rows[offset], *later)
        else:
            (block,) = add(got[offset], here, at_rows[offset])
        sent.append(swap(block, offset))
    sent += [swap(later[0], close ^ 2), swap(later[1], 2), later[2]]
    mine = here[at_rows[0] :].astype(jnp.float32)
    for block in sent:
        mine = mine + block.astype(jnp.float32)
    if tp > 1:
        mine = lax.psum_scatter(mine, "tp", scatter_dimension=0, tiled=True)
    return (resid.astype(jnp.float32) + mine).astype(jnp.bfloat16)


def solution(mesh):
    return jax.shard_map(
        shards,
        mesh=mesh,
        in_specs=(
            P(("parts", "ep", "tp"), None),
            P(),
            P(("parts", "ep"), None),
            P(("parts", "ep"), None),
            P("ep", None, None, "tp"),
            P("ep", "tp", None),
        ),
        out_specs=P(("parts", "ep", "tp"), None),
        check_vma=False,
    )
```

```python
import functools

import jax
import jax.numpy as jnp
from jax import lax
from jax.experimental import pallas as pl
from jax.experimental.pallas import tpu as pltpu
from jax.sharding import PartitionSpec as P

eps = 1e-06
lane = 128
VMEM = pl.BlockSpec(memory_space=pltpu.VMEM)
ANY = pl.BlockSpec(memory_space=pl.ANY)
HBM = pl.BlockSpec(memory_space=pltpu.HBM)


def limit(mib):
    return pltpu.CompilerParams(vmem_limit_bytes=mib << 20)


def in_hbm(array):
    return pltpu.with_memory_space_constraint(array, pltpu.HBM)


def in_vmem(array):
    return pltpu.with_memory_space_constraint(array, pltpu.VMEM)


def norm_kernel(*refs):
    sources, out_ref, held, sems = refs[:4], refs[4], refs[5:9], refs[9]
    copies = [
        pltpu.make_async_copy(source, ref, sems.at[i])
        for i, (source, ref) in enumerate(zip(sources, held))
    ]
    for copy in copies:
        copy.start()
    for copy in copies:
        copy.wait()
    resid_ref, gain_ref, ids_ref, weights_ref = held
    rows, width = resid_ref.shape
    values = resid_ref[...].astype(jnp.float32)
    scale = lax.rsqrt(jnp.mean(values * values, axis=-1, keepdims=True) + eps)
    gain = gain_ref[...].reshape(1, width)
    out_ref[:, :width] = (values * scale * gain).astype(jnp.bfloat16)
    chosen, count = ids_ref.shape
    experts = lax.broadcasted_iota(jnp.int32, (lane, count), 0)
    share = jnp.zeros((lane, count), jnp.float32)
    for k in range(chosen):
        weight = weights_ref[k : k + 1, :].astype(jnp.float32)
        share = share + jnp.where(experts == ids_ref[k : k + 1, :], weight, 0.0)
    out_ref[:, width:] = share.T.astype(jnp.bfloat16)


def norm(resid, gain, ids, weights):
    rows, width = resid.shape
    sources = [resid, gain, ids.T, weights.T]
    return pl.pallas_call(
        norm_kernel,
        out_shape=jax.ShapeDtypeStruct((rows, width + lane), jnp.bfloat16),
        in_specs=[HBM] * 4,
        out_specs=VMEM,
        scratch_shapes=[pltpu.VMEM(a.shape, a.dtype) for a in sources]
        + [pltpu.SemaphoreType.DMA((4,))],
        compiler_params=limit(3),
        name="norm",
    )(*[in_hbm(a) for a in sources])


def unpack_kernel(first, packed_ref, *refs):
    out_ref, token_ref, buffer, sems = refs[-4:]
    token_ref[...] = jnp.zeros_like(token_ref)
    width = packed_ref.shape[1]
    groups = buffer.shape[0]
    inner = groups * lane
    copies = [
        pltpu.make_async_copy(
            packed_ref.at[0, :, :, (first + c) * lane : (first + c + 1) * lane],
            buffer.at[c],
            sems.at[c],
        )
        for c in range(groups)
    ]
    for copy in copies:
        copy.start()
    tile = 128
    for c in range(groups):
        copies[c].wait()
        rows = buffer.at[c].reshape(2 * width, lane)

        def step(i, _):
            both = rows.at[pl.ds(pl.multiple_of(i * 2 * tile, 2 * tile), 2 * tile), :]
            to = pl.ds(pl.multiple_of(i * tile, tile), tile)
            out_ref[to, c * lane : (c + 1) * lane] = both[pl.ds(0, tile, stride=2), :]
            out_ref[to, inner + c * lane : inner + (c + 1) * lane] = both[
                pl.ds(1, tile, stride=2), :
            ]
            return 0

        lax.fori_loop(0, width // tile, step, 0, unroll=2)


def unpack(packed, first, groups, after, cost=0):
    width = packed.shape[1]
    return pl.pallas_call(
        functools.partial(unpack_kernel, first),
        out_shape=[
            jax.ShapeDtypeStruct((width, 2 * groups * lane), jnp.bfloat16),
            jax.ShapeDtypeStruct((8, lane), jnp.float32),
        ],
        in_specs=[HBM] + [ANY] * len(after),
        out_specs=[VMEM, VMEM],
        scratch_shapes=[
            pltpu.VMEM((groups, width, 2, lane), jnp.bfloat16),
            pltpu.SemaphoreType.DMA((groups,)),
        ],
        compiler_params=limit(9),
        cost_estimate=pl.CostEstimate(flops=0, bytes_accessed=cost, transcendentals=0),
        name="unpack",
    )(in_hbm(packed), *after)


def pass_kernel(*refs):
    count = (len(refs) - 1) // 2
    for source, out_ref in zip(refs[:count], refs[count + 1 :]):
        out_ref[...] = source[...]


def pass_on(blocks, after):
    return pl.pallas_call(
        pass_kernel,
        out_shape=[jax.ShapeDtypeStruct(b.shape, b.dtype) for b in blocks],
        in_specs=[VMEM] * len(blocks) + [ANY],
        out_specs=[VMEM] * len(blocks),
        compiler_params=limit(2),
        name="pass_on",
    )(*blocks, after)


def hidden_rows(rows_ref, gu_refs, hidden, at, tile):
    to = 0
    rows = rows_ref[at : at + tile, : gu_refs[0].shape[0]]
    for gu_ref in gu_refs:
        half = gu_ref.shape[1] // 2
        step = min(256, half)
        for n in range(0, half, step):
            gate = jnp.dot(rows, gu_ref[:, n : n + step], preferred_element_type=jnp.float32)
            up = jnp.dot(
                rows, gu_ref[:, half + n : half + n + step], preferred_element_type=jnp.float32
            )
            hidden[at : at + tile, to : to + step] = (jax.nn.silu(gate) * up).astype(jnp.bfloat16)
            to += step


def near_kernel(count, after, *refs):
    block_refs, gu_refs = refs[:count], refs[count : -2 - after]
    hidden, rows_ref = refs[-2:]
    size = block_refs[0].shape[0]
    for at, block_ref in enumerate(block_refs):
        rows_ref[at * size : (at + 1) * size, :] = block_ref[...]
    tile = min(256, size * count)
    for at in range(0, size * count, tile):
        hidden_rows(rows_ref, gu_refs, hidden, at, tile)


def near_hidden(blocks, halves, after):
    size, wide = blocks[0].shape
    count = size * len(blocks)
    width, inner = halves[0].shape[0], sum(h.shape[1] // 2 for h in halves)
    return pl.pallas_call(
        functools.partial(near_kernel, len(blocks), len(after)),
        out_shape=jax.ShapeDtypeStruct((count, inner), jnp.bfloat16),
        in_specs=[VMEM] * (len(blocks) + len(halves)) + [ANY] * len(after),
        out_specs=VMEM,
        scratch_shapes=[pltpu.VMEM((count, wide), jnp.bfloat16)],
        compiler_params=limit(6),
        cost_estimate=pl.CostEstimate(flops=0, bytes_accessed=0, transcendentals=0),
        name="near",
    )(*blocks, *halves, *after)


def down_rows(hidden, share, down_ref, out_ref):
    count, width = out_ref.shape
    tile = min(256, count)
    step = 512
    for at in range(0, count, tile):
        for n in range(0, width, step):
            piece = jnp.dot(
                hidden[at : at + tile, :],
                down_ref[0, :, n : n + step],
                preferred_element_type=jnp.float32,
            )
            piece = piece.astype(jnp.bfloat16).astype(jnp.float32)
            terms = (share[at : at + tile, :1] * piece).astype(jnp.bfloat16)
            out_ref[at : at + tile, n : n + step] = terms


def away_kernel(near_count, far_count, order, down_ref, near_hidden_ref, *refs):
    near_refs, far_refs = refs[:near_count], refs[near_count : near_count + far_count]
    gu_refs = refs[near_count + far_count : -6]
    away_ref, here_hidden, here_share, rows_ref, far_hidden, away_hidden = refs[-6:]
    width = down_ref.shape[2]
    size = near_refs[0].shape[0]
    for at, block_ref in enumerate(far_refs):
        rows_ref[at * size : (at + 1) * size, :] = block_ref[...]
    tile = min(256, size * far_count)
    for at in range(0, size * far_count, tile):
        hidden_rows(rows_ref, gu_refs, far_hidden, at, tile)
    half = len(order) // 2
    lanes = lax.broadcasted_iota(jnp.int32, (size, lane), 1)
    parts = []
    for to, (near, at) in enumerate(order):
        source = near_hidden_ref if near else far_hidden
        block = (near_refs if near else far_refs)[at][:, width:].astype(jnp.float32)
        mine = jnp.where(lanes == lax.axis_index("ep"), block, 0.0)
        share = jnp.sum(mine, axis=1, keepdims=True)
        place = slice(to % half * size, (to % half + 1) * size)
        if to < half:
            away_hidden[place, :] = source[at * size : (at + 1) * size, :]
            parts.append(share)
        else:
            here_hidden[place, :] = source[at * size : (at + 1) * size, :]
            here_share[place, :] = jnp.broadcast_to(share, (size, lane))
    down_rows(away_hidden, jnp.concatenate(parts, axis=0), down_ref, away_ref)


def here_kernel(down_ref, hidden_ref, share_ref, out_ref):
    down_rows(hidden_ref, share_ref, down_ref, out_ref)


def expert(down, hidden, near, far, halves, order):
    size = near[0].shape[0]
    count = size * (len(near) + len(far))
    half = count // 2
    _, inner, width = down.shape
    shape = jax.ShapeDtypeStruct
    away, here_hidden, here_share = pl.pallas_call(
        functools.partial(away_kernel, len(near), len(far), order),
        out_shape=[
            shape((half, width), jnp.bfloat16),
            shape((half, inner), jnp.bfloat16),
            shape((half, lane), jnp.float32),
        ],
        in_specs=[VMEM] * (2 + len(near) + len(far) + len(halves)),
        out_specs=[VMEM] * 3,
        scratch_shapes=[
            pltpu.VMEM((size * len(far), width + lane), jnp.bfloat16),
            pltpu.VMEM((size * len(far), inner), jnp.bfloat16),
            pltpu.VMEM((half, inner), jnp.bfloat16),
        ],
        compiler_params=limit(8 if count <= 256 else 24),
        cost_estimate=pl.CostEstimate(
            flops=3 * count * width * inner, bytes_accessed=0, transcendentals=count * inner // 2
        ),
        name="away",
    )(down, hidden, *near, *far, *halves)
    here = pl.pallas_call(
        here_kernel,
        out_shape=shape((half, width), jnp.bfloat16),
        in_specs=[VMEM] * 3,
        out_specs=VMEM,
        compiler_params=limit(4 if count <= 256 else 8),
        cost_estimate=pl.CostEstimate(
            flops=count * width * inner, bytes_accessed=0, transcendentals=0
        ),
        name="here",
    )(down, here_hidden, here_share)
    return away, here


def add_kernel(pieces, got_ref, here_ref, *refs):
    later = (len(refs) - len(pieces)) // 2
    for piece, out_ref in zip(pieces, refs[later:]):
        to = 0
        for rows, columns in piece:
            here = here_ref[slice(*rows), slice(*columns)].astype(jnp.float32)
            got = got_ref[slice(*rows), slice(*columns)].astype(jnp.float32)
            end = to + columns[1] - columns[0]
            out_ref[:, to:end] = (got + here).astype(jnp.bfloat16)
            to = end
    for source, out_ref in zip(refs, refs[len(refs) - later :]):
        out_ref[...] = source[...]


def add(got, here, pieces, later=()):
    shapes = [(piece[0][0][1] - piece[0][0][0], sum(c[1] - c[0] for _, c in piece)) for piece in pieces]
    shapes += [array.shape for array in later]
    return pl.pallas_call(
        functools.partial(add_kernel, tuple(tuple(piece) for piece in pieces)),
        out_shape=[jax.ShapeDtypeStruct(shape, jnp.bfloat16) for shape in shapes],
        in_specs=[VMEM] * (2 + len(later)),
        out_specs=[VMEM] * len(shapes),
        compiler_params=limit(2 if got.shape[0] <= 16 else 6 if got.shape[0] <= 128 else 16),
        name="add",
    )(got, here, *later)


def swap(block, offset):
    count = lax.axis_size("ep")
    return lax.ppermute(block, "ep", [(i, i ^ offset) for i in range(count)])


def gather_blocks(block, far, gate_up):
    groups = gate_up.shape[3] // lane // 2
    near = {0: block}
    lead, *late = far[:0:-1]
    close = far[0]
    near[lead], near[2] = swap(block, lead), swap(block, 2)
    first, token = unpack(gate_up, 0, groups, [], 1 << 24)
    (again,) = pass_on([block], token)
    for offset in (*late, close, close ^ 2):
        near[offset] = swap(again, offset)
    (near[lead],) = pass_on([near[lead]], near[2])
    near[lead ^ 2] = swap(near[lead], 2)
    second, token = unpack(gate_up, groups, gate_up.shape[3] // lane - groups, [again], 1 << 24)
    first_late = (lead, lead ^ 2, *late)
    near[lead], near[lead ^ 2], *held = pass_on([near[offset] for offset in first_late], token)
    for offset, array in zip(late, held):
        near[offset] = array
        near[offset ^ 2] = swap(array, 2)
    ready = (0, 2, close, close ^ 2)
    near[lead ^ 1] = swap(near[lead], 1)
    for offset, array in zip(ready, pass_on([near[offset] for offset in ready], near[lead ^ 1])):
        near[offset] = array
    for offset in (*ready, lead ^ 2, *late):
        near[offset ^ 1] = swap(near[offset], 1)
    for offset in late:
        near[offset ^ 3] = swap(near[offset ^ 2], 1)
    hidden = near_hidden(
        [near[offset] for offset in range(8)], [first, second], [near[late[-1] ^ 2]]
    )
    return near, [first, second], hidden


def shards(resid, norm_gain, expert_ids, route_weights, gate_up, down):
    owners = lax.axis_size("ep")
    tp = lax.axis_size("tp")
    far = tuple(range(4, owners, 4))
    resid_all = lax.all_gather(resid, "tp", axis=0, tiled=True) if tp > 1 else resid
    normed = norm(resid_all, norm_gain, expert_ids, route_weights)
    rows = normed.shape[0]
    blocks, parts, hidden = gather_blocks(normed, far, gate_up)
    order = sorted(blocks, key=lambda o: (1 - (o & 1), 1 - (o >> 1 & 1), -o))
    places = [(o < 8, o % 8 if o < 8 else o - 8) for o in order]
    near, late = [blocks[o] for o in range(8)], [blocks[o] for o in range(8, owners)]
    away, here = expert(down, hidden, near, late, parts, places)
    lead, *late = far[:0:-1]
    close = far[0]
    width = away.shape[1]
    cut = width // lane * 4 // 8 * lane
    keys = [o for o in order if o & 3 == 0]
    half = len(keys) * rows
    away_rows = {o: (at * rows, at * rows + rows) for at, o in enumerate(keys)}
    here_rows = {o: (half + at * rows, half + at * rows + rows) for at, o in enumerate(keys)}
    full, low, high = (0, width), (0, cut), (cut, width)
    pieces = {}
    for name, table in (("away", away_rows), ("here", here_rows)):
        pieces[name] = [(table[lead], full), *((table[o], low) for o in late)]
        pieces.update({(name, o): [(table[o], high)] for o in late})
        pieces.update({(name, o): [(table[o], full)] for o in (close, 0)})
    sums = dict(zip(pieces, add(swap(away, 1), here, list(pieces.values()))))
    got = swap(sums["away"], 2)
    direct = [swap(sums["here", o], o) for o in late]
    direct += [swap(sums["away", o], o ^ 2) for o in late]
    whole = [sums["here", 0], swap(sums["here", close], close)]
    whole.append(swap(sums["away", close], close ^ 2))
    later = [sums["away", 0]]
    ends = [width + at * cut for at in range(len(late) + 1)]
    parts = [full, *zip(ends, ends[1:])]
    total, *lows, own = add(got, sums["here"], [[((0, rows), part)] for part in parts], later)
    whole.append(swap(total, lead))
    summed = [swap(array, o) for o, array in zip(late, lows)]
    whole.append(swap(own, 2))
    mine = sum(array.astype(jnp.float32) for array in whole)
    halves = [sum(array.astype(jnp.float32) for array in part) for part in (summed, direct)]
    mine = mine + jnp.concatenate(halves, axis=1)
    if tp > 1:
        mine = lax.psum_scatter(mine, "tp", scatter_dimension=0, tiled=True)
    return (resid.astype(jnp.float32) + mine).astype(jnp.bfloat16)


def solution(mesh):
    return jax.shard_map(
        shards,
        mesh=mesh,
        in_specs=(
            P(("parts", "ep", "tp"), None),
            P(),
            P(("parts", "ep"), None),
            P(("parts", "ep"), None),
            P("ep", None, None, "tp"),
            P("ep", "tp", None),
        ),
        out_specs=P(("parts", "ep", "tp"), None),
        check_vma=False,
    )
```

```python
import functools

import jax
import jax.numpy as jnp
from jax import lax
from jax.experimental import pallas as pl
from jax.experimental.pallas import tpu as pltpu
from jax.sharding import PartitionSpec as P

eps = 1e-06
lane = 128
VMEM = pl.BlockSpec(memory_space=pltpu.VMEM)
ANY = pl.BlockSpec(memory_space=pl.ANY)
HBM = pl.BlockSpec(memory_space=pltpu.HBM)


def limit(mib):
    return pltpu.CompilerParams(vmem_limit_bytes=mib << 20)


def in_hbm(array):
    return pltpu.with_memory_space_constraint(array, pltpu.HBM)


def in_vmem(array):
    return pltpu.with_memory_space_constraint(array, pltpu.VMEM)


def norm_kernel(*refs):
    sources, out_ref, held, sems = refs[:4], refs[4], refs[5:9], refs[9]
    copies = [
        pltpu.make_async_copy(source, ref, sems.at[i])
        for i, (source, ref) in enumerate(zip(sources, held))
    ]
    for copy in copies:
        copy.start()
    for copy in copies:
        copy.wait()
    resid_ref, gain_ref, ids_ref, weights_ref = held
    rows, width = resid_ref.shape
    values = resid_ref[...].astype(jnp.float32)
    scale = lax.rsqrt(jnp.mean(values * values, axis=-1, keepdims=True) + eps)
    gain = gain_ref[...].reshape(1, width)
    out_ref[:, :width] = (values * scale * gain).astype(jnp.bfloat16)
    chosen, count = ids_ref.shape
    experts = lax.broadcasted_iota(jnp.int32, (lane, count), 0)
    share = jnp.zeros((lane, count), jnp.float32)
    for k in range(chosen):
        weight = weights_ref[k : k + 1, :].astype(jnp.float32)
        share = share + jnp.where(experts == ids_ref[k : k + 1, :], weight, 0.0)
    out_ref[:, width:] = share.T.astype(jnp.bfloat16)


def norm(resid, gain, ids, weights):
    rows, width = resid.shape
    sources = [resid, gain, ids.T, weights.T]
    return pl.pallas_call(
        norm_kernel,
        out_shape=jax.ShapeDtypeStruct((rows, width + lane), jnp.bfloat16),
        in_specs=[HBM] * 4,
        out_specs=VMEM,
        scratch_shapes=[pltpu.VMEM(a.shape, a.dtype) for a in sources]
        + [pltpu.SemaphoreType.DMA((4,))],
        compiler_params=limit(3),
        name="norm",
    )(*[in_hbm(a) for a in sources])


def unpack_kernel(first, packed_ref, *refs):
    out_ref, token_ref, buffer, sems = refs[-4:]
    token_ref[...] = jnp.zeros_like(token_ref)
    width = packed_ref.shape[1]
    groups = buffer.shape[0]
    inner = groups * lane
    copies = [
        pltpu.make_async_copy(
            packed_ref.at[0, :, :, (first + c) * lane : (first + c + 1) * lane],
            buffer.at[c],
            sems.at[c],
        )
        for c in range(groups)
    ]
    for copy in copies:
        copy.start()
    tile = 128
    for c in range(groups):
        copies[c].wait()
        rows = buffer.at[c].reshape(2 * width, lane)

        def step(i, _):
            both = rows.at[pl.ds(pl.multiple_of(i * 2 * tile, 2 * tile), 2 * tile), :]
            to = pl.ds(pl.multiple_of(i * tile, tile), tile)
            out_ref[to, c * lane : (c + 1) * lane] = both[pl.ds(0, tile, stride=2), :]
            out_ref[to, inner + c * lane : inner + (c + 1) * lane] = both[
                pl.ds(1, tile, stride=2), :
            ]
            return 0

        lax.fori_loop(0, width // tile, step, 0, unroll=2)


def unpack(packed, first, groups, after, cost=0):
    width = packed.shape[1]
    return pl.pallas_call(
        functools.partial(unpack_kernel, first),
        out_shape=[
            jax.ShapeDtypeStruct((width, 2 * groups * lane), jnp.bfloat16),
            jax.ShapeDtypeStruct((8, lane), jnp.float32),
        ],
        in_specs=[HBM] + [ANY] * len(after),
        out_specs=[VMEM, VMEM],
        scratch_shapes=[
            pltpu.VMEM((groups, width, 2, lane), jnp.bfloat16),
            pltpu.SemaphoreType.DMA((groups,)),
        ],
        compiler_params=limit(9),
        cost_estimate=pl.CostEstimate(flops=0, bytes_accessed=cost, transcendentals=0),
        name="unpack",
    )(in_hbm(packed), *after)


def join_kernel(sizes, *refs):
    sources, out_refs = refs[: sum(sizes)], refs[-len(sizes) :]
    at = 0
    for size, out_ref in zip(sizes, out_refs):
        to = 0
        for source in sources[at : at + size]:
            rows = source.shape[0]
            out_ref[to : to + rows, :] = source[...]
            to += rows
        at += size


def join(groups, after):
    blocks = [block for group in groups for block in group]
    shapes = [(sum(b.shape[0] for b in group), group[0].shape[1]) for group in groups]
    return pl.pallas_call(
        functools.partial(join_kernel, tuple(len(group) for group in groups)),
        out_shape=[jax.ShapeDtypeStruct(shape, jnp.bfloat16) for shape in shapes],
        in_specs=[VMEM] * len(blocks) + [ANY] * len(after),
        out_specs=[VMEM] * len(groups),
        compiler_params=limit(4 if len(blocks) < 8 else 12),
        name="join",
    )(*blocks, *after)


def hidden_rows(rows_ref, gu_refs, hidden, at, tile):
    to = 0
    rows = rows_ref[at : at + tile, : gu_refs[0].shape[0]]
    for gu_ref in gu_refs:
        half = gu_ref.shape[1] // 2
        step = min(256, half)
        for n in range(0, half, step):
            gate = jnp.dot(rows, gu_ref[:, n : n + step], preferred_element_type=jnp.float32)
            up = jnp.dot(
                rows, gu_ref[:, half + n : half + n + step], preferred_element_type=jnp.float32
            )
            hidden[at : at + tile, to : to + step] = (jax.nn.silu(gate) * up).astype(jnp.bfloat16)
            to += step


def fill(rows_ref, block_refs):
    to = 0
    for block_ref in block_refs:
        rows = block_ref.shape[0]
        rows_ref[to : to + rows, :] = block_ref[...]
        to += rows


def hidden_and_share(rows_ref, gu_refs, hidden, share_ref):
    rows = rows_ref.shape[0]
    width = gu_refs[0].shape[0]
    tile = min(256, rows)
    for at in range(0, rows, tile):
        hidden_rows(rows_ref, gu_refs, hidden, at, min(tile, rows - at))
    shares = rows_ref[:, width:].astype(jnp.float32)
    lanes = lax.broadcasted_iota(jnp.int32, shares.shape, 1)
    mine = jnp.where(lanes == lax.axis_index("ep"), shares, 0.0)
    share_ref[...] = jnp.broadcast_to(jnp.sum(mine, axis=1, keepdims=True), shares.shape)


def hidden_kernel(count, after, *refs):
    block_refs, gu_refs = refs[:count], refs[count : -3 - after]
    hidden, share_ref, rows_ref = refs[-3:]
    fill(rows_ref, block_refs)
    hidden_and_share(rows_ref, gu_refs, hidden, share_ref)


def hidden_of(blocks, halves, after):
    count, wide = sum(b.shape[0] for b in blocks), blocks[0].shape[1]
    width, inner = halves[0].shape[0], sum(h.shape[1] // 2 for h in halves)
    return pl.pallas_call(
        functools.partial(hidden_kernel, len(blocks), len(after)),
        out_shape=[
            jax.ShapeDtypeStruct((count, inner), jnp.bfloat16),
            jax.ShapeDtypeStruct((count, lane), jnp.float32),
        ],
        in_specs=[VMEM] * (len(blocks) + len(halves)) + [ANY] * len(after),
        out_specs=[VMEM, VMEM],
        scratch_shapes=[pltpu.VMEM((count, wide), jnp.bfloat16)],
        compiler_params=limit(6 if count <= 256 else 16),
        cost_estimate=pl.CostEstimate(flops=0, bytes_accessed=0, transcendentals=0),
        name="hidden",
    )(*blocks, *halves, *after)


def down_rows(hidden, share, down_ref, out_ref):
    count, width = out_ref.shape
    tile = min(256, count)
    step = 512
    for at in range(0, count, tile):
        for n in range(0, width, step):
            piece = jnp.dot(
                hidden[at : at + tile, :],
                down_ref[0, :, n : n + step],
                preferred_element_type=jnp.float32,
            )
            piece = piece.astype(jnp.bfloat16).astype(jnp.float32)
            terms = (share[at : at + tile, :1] * piece).astype(jnp.bfloat16)
            out_ref[at : at + tile, n : n + step] = terms


def away_kernel(sets, count, places, down_ref, *refs):
    hidden_refs, share_refs, refs = refs[:sets], refs[sets : 2 * sets], refs[2 * sets :]
    block_refs, gu_refs = refs[:count], refs[count:-7]
    away_ref, here_hidden, here_share, last_rows, last_hidden, last_share, hidden = refs[-7:]
    half = away_ref.shape[0]
    size = 2 * half // len(places)
    fill(last_rows, block_refs)
    hidden_and_share(last_rows, gu_refs, last_hidden, last_share)
    hidden_refs = (*hidden_refs, last_hidden)
    share_refs = (*share_refs, last_share)
    shares = []
    for to, (which, at) in enumerate(places):
        part = slice(at, at + size)
        place = slice(to * size % half, to * size % half + size)
        if to * size < half:
            hidden[place, :] = hidden_refs[which][part, :]
            shares.append(share_refs[which][part, :])
        else:
            here_hidden[place, :] = hidden_refs[which][part, :]
            here_share[place, :] = share_refs[which][part, :]
    down_rows(hidden, jnp.concatenate(shares, axis=0), down_ref, away_ref)


def here_kernel(down_ref, hidden_ref, share_ref, out_ref):
    down_rows(hidden_ref, share_ref, down_ref, out_ref)


def expert(down, hidden, shares, last, halves, places, rows):
    half = rows * len(places) // 2
    last_count = sum(b.shape[0] for b in last)
    _, inner, width = down.shape
    shape = jax.ShapeDtypeStruct
    away, here_hidden, here_share = pl.pallas_call(
        functools.partial(away_kernel, len(hidden), len(last), tuple(places)),
        out_shape=[
            shape((half, width), jnp.bfloat16),
            shape((half, inner), jnp.bfloat16),
            shape((half, lane), jnp.float32),
        ],
        in_specs=[VMEM] * (1 + 2 * len(hidden) + len(last) + len(halves)),
        out_specs=[VMEM] * 3,
        scratch_shapes=[
            pltpu.VMEM((last_count, width + lane), jnp.bfloat16),
            pltpu.VMEM((last_count, inner), jnp.bfloat16),
            pltpu.VMEM((last_count, lane), jnp.float32),
            pltpu.VMEM((half, inner), jnp.bfloat16),
        ],
        compiler_params=limit(8 if half <= 128 else 24),
        cost_estimate=pl.CostEstimate(
            flops=6 * half * width * inner, bytes_accessed=0, transcendentals=half * inner
        ),
        name="away",
    )(down, *hidden, *shares, *last, *halves)
    here = pl.pallas_call(
        here_kernel,
        out_shape=shape((half, width), jnp.bfloat16),
        in_specs=[VMEM] * 3,
        out_specs=VMEM,
        compiler_params=limit(4 if half <= 128 else 8),
        cost_estimate=pl.CostEstimate(
            flops=2 * half * width * inner, bytes_accessed=0, transcendentals=0
        ),
        name="here",
    )(down, here_hidden, here_share)
    return away, here


def add_kernel(pieces, got_ref, here_ref, *refs):
    later = (len(refs) - len(pieces)) // 2
    for piece, out_ref in zip(pieces, refs[later:]):
        to = 0
        for rows, columns in piece:
            here = here_ref[slice(*rows), slice(*columns)].astype(jnp.float32)
            got = got_ref[slice(*rows), slice(*columns)].astype(jnp.float32)
            end = to + columns[1] - columns[0]
            out_ref[:, to:end] = (got + here).astype(jnp.bfloat16)
            to = end
    for source, out_ref in zip(refs, refs[len(refs) - later :]):
        out_ref[...] = source[...]


def add(got, here, pieces, later=()):
    shapes = [(piece[0][0][1] - piece[0][0][0], sum(c[1] - c[0] for _, c in piece)) for piece in pieces]
    shapes += [array.shape for array in later]
    return pl.pallas_call(
        functools.partial(add_kernel, tuple(tuple(piece) for piece in pieces)),
        out_shape=[jax.ShapeDtypeStruct(shape, jnp.bfloat16) for shape in shapes],
        in_specs=[VMEM] * (2 + len(later)),
        out_specs=[VMEM] * len(shapes),
        compiler_params=limit(2 if got.shape[0] <= 16 else 6 if got.shape[0] <= 128 else 16),
        name="add",
    )(got, here, *later)


def swap(block, offset):
    count = lax.axis_size("ep")
    return lax.ppermute(block, "ep", [(i, i ^ offset) for i in range(count)])


def join_kernel(sizes, *refs):
    sources, out_refs = refs[: sum(sizes)], refs[-len(sizes) :]
    at = 0
    for size, out_ref in zip(sizes, out_refs):
        to = 0
        for source in sources[at : at + size]:
            rows = source.shape[0]
            out_ref[to : to + rows, :] = source[...]
            to += rows
        at += size


def join(groups, after):
    blocks = [block for group in groups for block in group]
    shapes = [(sum(b.shape[0] for b in group), group[0].shape[1]) for group in groups]
    return pl.pallas_call(
        functools.partial(join_kernel, tuple(len(group) for group in groups)),
        out_shape=[jax.ShapeDtypeStruct(shape, jnp.bfloat16) for shape in shapes],
        in_specs=[VMEM] * len(blocks) + [ANY] * len(after),
        out_specs=[VMEM] * len(groups),
        compiler_params=limit(4 if len(blocks) < 8 else 12),
        name="join",
    )(*blocks, *after)


def hidden_rows(rows_ref, gu_refs, hidden, at, tile):
    to = 0
    rows = rows_ref[at : at + tile, : gu_refs[0].shape[0]]
    for gu_ref in gu_refs:
        half = gu_ref.shape[1] // 2
        step = min(256, half)
        for n in range(0, half, step):
            gate = jnp.dot(rows, gu_ref[:, n : n + step], preferred_element_type=jnp.float32)
            up = jnp.dot(
                rows, gu_ref[:, half + n : half + n + step], preferred_element_type=jnp.float32
            )
            hidden[at : at + tile, to : to + step] = (jax.nn.silu(gate) * up).astype(jnp.bfloat16)
            to += step


def fill(rows_ref, block_refs):
    to = 0
    for block_ref in block_refs:
        rows = block_ref.shape[0]
        rows_ref[to : to + rows, :] = block_ref[...]
        to += rows


def hidden_and_share(rows_ref, gu_refs, hidden, share_ref):
    rows = rows_ref.shape[0]
    width = gu_refs[0].shape[0]
    tile = min(256, rows)
    for at in range(0, rows, tile):
        hidden_rows(rows_ref, gu_refs, hidden, at, min(tile, rows - at))
    shares = rows_ref[:, width:].astype(jnp.float32)
    lanes = lax.broadcasted_iota(jnp.int32, shares.shape, 1)
    mine = jnp.where(lanes == lax.axis_index("ep"), shares, 0.0)
    share_ref[...] = jnp.broadcast_to(jnp.sum(mine, axis=1, keepdims=True), shares.shape)


def hidden_kernel(count, after, *refs):
    block_refs, gu_refs = refs[:count], refs[count : -3 - after]
    hidden, share_ref, rows_ref = refs[-3:]
    fill(rows_ref, block_refs)
    hidden_and_share(rows_ref, gu_refs, hidden, share_ref)


def hidden_of(blocks, halves, after):
    count, wide = sum(b.shape[0] for b in blocks), blocks[0].shape[1]
    width, inner = halves[0].shape[0], sum(h.shape[1] // 2 for h in halves)
    return pl.pallas_call(
        functools.partial(hidden_kernel, len(blocks), len(after)),
        out_shape=[
            jax.ShapeDtypeStruct((count, inner), jnp.bfloat16),
            jax.ShapeDtypeStruct((count, lane), jnp.float32),
        ],
        in_specs=[VMEM] * (len(blocks) + len(halves)) + [ANY] * len(after),
        out_specs=[VMEM, VMEM],
        scratch_shapes=[pltpu.VMEM((count, wide), jnp.bfloat16)],
        compiler_params=limit(6 if count <= 256 else 16),
        cost_estimate=pl.CostEstimate(flops=0, bytes_accessed=0, transcendentals=0),
        name="hidden",
    )(*blocks, *halves, *after)


def down_rows(hidden, share, down_ref, out_ref):
    count, width = out_ref.shape
    tile = min(256, count)
    step = 512
    for at in range(0, count, tile):
        for n in range(0, width, step):
            piece = jnp.dot(
                hidden[at : at + tile, :],
                down_ref[0, :, n : n + step],
                preferred_element_type=jnp.float32,
            )
            piece = piece.astype(jnp.bfloat16).astype(jnp.float32)
            terms = (share[at : at + tile, :1] * piece).astype(jnp.bfloat16)
            out_ref[at : at + tile, n : n + step] = terms


def away_kernel(sets, count, places, down_ref, *refs):
    hidden_refs, share_refs, refs = refs[:sets], refs[sets : 2 * sets], refs[2 * sets :]
    block_refs, gu_refs = refs[:count], refs[count:-7]
    away_ref, here_hidden, here_share, last_rows, last_hidden, last_share, hidden = refs[-7:]
    half = away_ref.shape[0]
    size = 2 * half // len(places)
    fill(last_rows, block_refs)
    hidden_and_share(last_rows, gu_refs, last_hidden, last_share)
    hidden_refs = (*hidden_refs, last_hidden)
    share_refs = (*share_refs, last_share)
    shares = []
    for to, (which, at) in enumerate(places):
        part = slice(at, at + size)
        place = slice(to * size % half, to * size % half + size)
        if to * size < half:
            hidden[place, :] = hidden_refs[which][part, :]
            shares.append(share_refs[which][part, :])
        else:
            here_hidden[place, :] = hidden_refs[which][part, :]
            here_share[place, :] = share_refs[which][part, :]
    down_rows(hidden, jnp.concatenate(shares, axis=0), down_ref, away_ref)


def here_kernel(down_ref, hidden_ref, share_ref, out_ref):
    down_rows(hidden_ref, share_ref, down_ref, out_ref)


def expert(down, hidden, shares, last, halves, places, rows):
    half = rows * len(places) // 2
    last_count = sum(b.shape[0] for b in last)
    _, inner, width = down.shape
    shape = jax.ShapeDtypeStruct
    away, here_hidden, here_share = pl.pallas_call(
        functools.partial(away_kernel, len(hidden), len(last), tuple(places)),
        out_shape=[
            shape((half, width), jnp.bfloat16),
            shape((half, inner), jnp.bfloat16),
            shape((half, lane), jnp.float32),
        ],
        in_specs=[VMEM] * (1 + 2 * len(hidden) + len(last) + len(halves)),
        out_specs=[VMEM] * 3,
        scratch_shapes=[
            pltpu.VMEM((last_count, width + lane), jnp.bfloat16),
            pltpu.VMEM((last_count, inner), jnp.bfloat16),
            pltpu.VMEM((last_count, lane), jnp.float32),
            pltpu.VMEM((half, inner), jnp.bfloat16),
        ],
        compiler_params=limit(8 if half <= 128 else 24),
        cost_estimate=pl.CostEstimate(
            flops=6 * half * width * inner, bytes_accessed=0, transcendentals=half * inner
        ),
        name="away",
    )(down, *hidden, *shares, *last, *halves)
    here = pl.pallas_call(
        here_kernel,
        out_shape=shape((half, width), jnp.bfloat16),
        in_specs=[VMEM] * 3,
        out_specs=VMEM,
        compiler_params=limit(4 if half <= 128 else 8),
        cost_estimate=pl.CostEstimate(
            flops=2 * half * width * inner, bytes_accessed=0, transcendentals=0
        ),
        name="here",
    )(down, here_hidden, here_share)
    return away, here


def add_kernel(pieces, got_ref, here_ref, *refs):
    later = (len(refs) - len(pieces)) // 2
    for piece, out_ref in zip(pieces, refs[later:]):
        to = 0
        for rows, columns in piece:
            here = here_ref[slice(*rows), slice(*columns)].astype(jnp.float32)
            got = got_ref[slice(*rows), slice(*columns)].astype(jnp.float32)
            end = to + columns[1] - columns[0]
            out_ref[:, to:end] = (got + here).astype(jnp.bfloat16)
            to = end
    for source, out_ref in zip(refs, refs[len(refs) - later :]):
        out_ref[...] = source[...]


def add(got, here, pieces, later=()):
    shapes = [(piece[0][0][1] - piece[0][0][0], sum(c[1] - c[0] for _, c in piece)) for piece in pieces]
    shapes += [array.shape for array in later]
    return pl.pallas_call(
        functools.partial(add_kernel, tuple(tuple(piece) for piece in pieces)),
        out_shape=[jax.ShapeDtypeStruct(shape, jnp.bfloat16) for shape in shapes],
        in_specs=[VMEM] * (2 + len(later)),
        out_specs=[VMEM] * len(shapes),
        compiler_params=limit(2 if got.shape[0] <= 16 else 6 if got.shape[0] <= 128 else 16),
        name="add",
    )(got, here, *later)


def swap(block, offset):
    count = lax.axis_size("ep")
    return lax.ppermute(block, "ep", [(i, i ^ offset) for i in range(count)])


def gather_blocks(block, far, gate_up):
    groups = gate_up.shape[3] // lane // 2
    lead, *late = far[:0:-1]
    close = far[0]
    along, beside = swap(block, lead), swap(block, 2)
    first, token = unpack(gate_up, 0, groups, [], 1 << 24)
    (again,) = join([[block]], [token])
    others = {offset: swap(again, offset) for offset in (*late, close, close ^ 2)}
    along, early = join([[along], [block, beside, along]], [beside])
    across = swap(along, 2)
    second, token = unpack(gate_up, groups, gate_up.shape[3] // lane - groups, [again], 1 << 24)
    halves = [first, second]
    middle, *held = join(
        [[across, *(others[o] for o in late)], *([others[o]] for o in late)], [token]
    )
    last = [swap(array, 2) for array in held]
    near = [early, middle, others[close], others[close ^ 2]]
    hidden, share = hidden_of(near, halves, [])
    *last, both = join([*([array] for array in last), near[2:]], [share])
    pairs = [swap(array, 1) for array in (*near[:2], both)]
    last = [*pairs, *last, *(swap(array, 1) for array in last)]
    keys = [0, 2, lead, lead ^ 2, *late, close, close ^ 2]
    ends = [o ^ 2 for o in late]
    keys = [keys, [*(o ^ 1 for o in keys), *ends, *(o ^ 1 for o in ends)]]
    return [hidden], [share], last, halves, keys


def shards(resid, norm_gain, expert_ids, route_weights, gate_up, down):
    owners = lax.axis_size("ep")
    tp = lax.axis_size("tp")
    far = tuple(range(4, owners, 4))
    resid_all = lax.all_gather(resid, "tp", axis=0, tiled=True) if tp > 1 else resid
    normed = norm(resid_all, norm_gain, expert_ids, route_weights)
    rows = normed.shape[0]
    hidden, shares, last, halves, keys = gather_blocks(normed, far, gate_up)
    order = sorted(range(owners), key=lambda o: (1 - (o & 1), 1 - (o >> 1 & 1), -o))
    found = {o: (which, at * rows) for which, part in enumerate(keys) for at, o in enumerate(part)}
    away, here = expert(down, hidden, shares, last, halves, [found[o] for o in order], rows)
    lead, *late = far[:0:-1]
    close = far[0]
    width = away.shape[1]
    cut = width // lane * 3 // 8 * lane
    keys = [o for o in order if o & 3 == 0]
    half = len(keys) * rows
    away_rows = {o: (at * rows, at * rows + rows) for at, o in enumerate(keys)}
    here_rows = {o: (half + at * rows, half + at * rows + rows) for at, o in enumerate(keys)}
    full, low, high = (0, width), (0, cut), (cut, width)
    pieces = {}
    for name, table in (("away", away_rows), ("here", here_rows)):
        pieces[name] = [(table[lead], full), *((table[o], low) for o in late)]
        pieces.update({(name, o): [(table[o], high)] for o in late})
        pieces.update({(name, o): [(table[o], full)] for o in (close, 0)})
    sums = dict(zip(pieces, add(swap(away, 1), here, list(pieces.values()))))
    got = swap(sums["away"], 2)
    direct = [swap(sums["here", o], o) for o in late]
    direct += [swap(sums["away", o], o ^ 2) for o in late]
    whole = [sums["here", 0], swap(sums["here", close], close)]
    whole.append(swap(sums["away", close], close ^ 2))
    later = [sums["away", 0]]
    ends = [width + at * cut for at in range(len(late) + 1)]
    parts = [full, *zip(ends, ends[1:])]
    total, *lows, own = add(got, sums["here"], [[((0, rows), part)] for part in parts], later)
    whole.append(swap(total, lead))
    summed = [swap(array, o) for o, array in zip(late, lows)]
    whole.append(swap(own, 2))
    mine = sum(array.astype(jnp.float32) for array in whole)
    halves = [sum(array.astype(jnp.float32) for array in part) for part in (summed, direct)]
    mine = mine + jnp.concatenate(halves, axis=1)
    if tp > 1:
        mine = lax.psum_scatter(mine, "tp", scatter_dimension=0, tiled=True)
    return (resid.astype(jnp.float32) + mine).astype(jnp.bfloat16)


def solution(mesh):
    return jax.shard_map(
        shards,
        mesh=mesh,
        in_specs=(
            P(("parts", "ep", "tp"), None),
            P(),
            P(("parts", "ep"), None),
            P(("parts", "ep"), None),
            P("ep", None, None, "tp"),
            P("ep", "tp", None),
        ),
        out_specs=P(("parts", "ep", "tp"), None),
        check_vma=False,
    )
```

```python
import functools

import jax
import jax.numpy as jnp
from jax import lax
from jax.experimental import pallas as pl
from jax.experimental.pallas import tpu as pltpu
from jax.sharding import PartitionSpec as P

eps = 1e-06
lane = 128
VMEM = pl.BlockSpec(memory_space=pltpu.VMEM)
ANY = pl.BlockSpec(memory_space=pl.ANY)
HBM = pl.BlockSpec(memory_space=pltpu.HBM)


def limit(mib):
    return pltpu.CompilerParams(vmem_limit_bytes=mib << 20)


def in_hbm(array):
    return pltpu.with_memory_space_constraint(array, pltpu.HBM)


def in_vmem(array):
    return pltpu.with_memory_space_constraint(array, pltpu.VMEM)


def norm_kernel(*refs):
    sources, out_ref, held, sems = refs[:4], refs[4], refs[5:9], refs[9]
    copies = [
        pltpu.make_async_copy(source, ref, sems.at[i])
        for i, (source, ref) in enumerate(zip(sources, held))
    ]
    for copy in copies:
        copy.start()
    for copy in copies:
        copy.wait()
    resid_ref, gain_ref, ids_ref, weights_ref = held
    rows, width = resid_ref.shape
    values = resid_ref[...].astype(jnp.float32)
    scale = lax.rsqrt(jnp.mean(values * values, axis=-1, keepdims=True) + eps)
    gain = gain_ref[...].reshape(1, width)
    out_ref[:, :width] = (values * scale * gain).astype(jnp.bfloat16)
    chosen, count = ids_ref.shape
    experts = lax.broadcasted_iota(jnp.int32, (lane, count), 0)
    share = jnp.zeros((lane, count), jnp.float32)
    for k in range(chosen):
        weight = weights_ref[k : k + 1, :].astype(jnp.float32)
        share = share + jnp.where(experts == ids_ref[k : k + 1, :], weight, 0.0)
    out_ref[:, width:] = share.T.astype(jnp.bfloat16)


def norm(resid, gain, ids, weights):
    rows, width = resid.shape
    sources = [resid, gain, ids.T, weights.T]
    return pl.pallas_call(
        norm_kernel,
        out_shape=jax.ShapeDtypeStruct((rows, width + lane), jnp.bfloat16),
        in_specs=[HBM] * 4,
        out_specs=VMEM,
        scratch_shapes=[pltpu.VMEM(a.shape, a.dtype) for a in sources]
        + [pltpu.SemaphoreType.DMA((4,))],
        compiler_params=limit(3),
        name="norm",
    )(*[in_hbm(a) for a in sources])


def unpack_kernel(first, packed_ref, *refs):
    out_ref, token_ref, buffer, sems = refs[-4:]
    token_ref[...] = jnp.zeros_like(token_ref)
    width = packed_ref.shape[1]
    groups = buffer.shape[0]
    inner = groups * lane
    cuts = sems.shape[1]
    depth = width // cuts
    copies = {
        (c, part): pltpu.make_async_copy(
            packed_ref.at[
                0,
                part * depth : (part + 1) * depth,
                :,
                (first + c) * lane : (first + c + 1) * lane,
            ],
            buffer.at[c, part * depth : (part + 1) * depth],
            sems.at[c, part],
        )
        for c in range(groups)
        for part in range(cuts)
    }
    for copy in copies.values():
        copy.start()
    tile = 128
    for (c, part), copy in copies.items():
        copy.wait()
        rows = buffer.at[c].reshape(2 * width, lane)

        def step(i, _):
            at = part * depth + i * tile
            both = rows.at[pl.ds(pl.multiple_of(2 * at, 2 * tile), 2 * tile), :]
            to = pl.ds(pl.multiple_of(at, tile), tile)
            out_ref[to, c * lane : (c + 1) * lane] = both[pl.ds(0, tile, stride=2), :]
            out_ref[to, inner + c * lane : inner + (c + 1) * lane] = both[
                pl.ds(1, tile, stride=2), :
            ]
            return 0

        lax.fori_loop(0, depth // tile, step, 0, unroll=7)


def unpack(packed, first, groups, after, cost=0):
    width = packed.shape[1]
    return pl.pallas_call(
        functools.partial(unpack_kernel, first),
        out_shape=[
            jax.ShapeDtypeStruct((width, 2 * groups * lane), jnp.bfloat16),
            jax.ShapeDtypeStruct((8, lane), jnp.float32),
        ],
        in_specs=[HBM] + [ANY] * len(after),
        out_specs=[VMEM, VMEM],
        scratch_shapes=[
            pltpu.VMEM((groups, width, 2, lane), jnp.bfloat16),
            pltpu.SemaphoreType.DMA((groups, 4)),
        ],
        compiler_params=limit(9),
        cost_estimate=pl.CostEstimate(flops=0, bytes_accessed=cost, transcendentals=0),
        name="unpack",
    )(in_hbm(packed), *after)


def join_kernel(sizes, *refs):
    sources, out_refs = refs[: sum(sizes)], refs[-len(sizes) :]
    at = 0
    for size, out_ref in zip(sizes, out_refs):
        to = 0
        for source in sources[at : at + size]:
            rows = source.shape[0]
            out_ref[to : to + rows, :] = source[...]
            to += rows
        at += size


def join(groups, after):
    blocks = [block for group in groups for block in group]
    shapes = [(sum(b.shape[0] for b in group), group[0].shape[1]) for group in groups]
    return pl.pallas_call(
        functools.partial(join_kernel, tuple(len(group) for group in groups)),
        out_shape=[jax.ShapeDtypeStruct(shape, jnp.bfloat16) for shape in shapes],
        in_specs=[VMEM] * len(blocks) + [ANY] * len(after),
        out_specs=[VMEM] * len(groups),
        compiler_params=limit(4 if len(blocks) < 8 else 12),
        name="join",
    )(*blocks, *after)


def hidden_rows(rows_ref, gu_refs, hidden, at, tile):
    to = 0
    rows = rows_ref[at : at + tile, : gu_refs[0].shape[0]]
    for gu_ref in gu_refs:
        half = gu_ref.shape[1] // 2
        step = min(256, half)
        for n in range(0, half, step):
            gate = jnp.dot(rows, gu_ref[:, n : n + step], preferred_element_type=jnp.float32)
            up = jnp.dot(
                rows, gu_ref[:, half + n : half + n + step], preferred_element_type=jnp.float32
            )
            hidden[at : at + tile, to : to + step] = (jax.nn.silu(gate) * up).astype(jnp.bfloat16)
            to += step


def fill(rows_ref, block_refs):
    to = 0
    for block_ref in block_refs:
        rows = block_ref.shape[0]
        rows_ref[to : to + rows, :] = block_ref[...]
        to += rows


def hidden_and_share(rows_ref, gu_refs, hidden, share_ref):
    rows = rows_ref.shape[0]
    width = gu_refs[0].shape[0]
    tile = min(256, rows)
    for at in range(0, rows, tile):
        hidden_rows(rows_ref, gu_refs, hidden, at, min(tile, rows - at))
    shares = rows_ref[:, width:].astype(jnp.float32)
    lanes = lax.broadcasted_iota(jnp.int32, shares.shape, 1)
    mine = jnp.where(lanes == lax.axis_index("ep"), shares, 0.0)
    share_ref[...] = jnp.broadcast_to(jnp.sum(mine, axis=1, keepdims=True), shares.shape)


def hidden_kernel(count, after, *refs):
    block_refs, gu_refs = refs[:count], refs[count : -3 - after]
    hidden, share_ref, rows_ref = refs[-3:]
    fill(rows_ref, block_refs)
    hidden_and_share(rows_ref, gu_refs, hidden, share_ref)


def hidden_of(blocks, halves, after):
    count, wide = sum(b.shape[0] for b in blocks), blocks[0].shape[1]
    width, inner = halves[0].shape[0], sum(h.shape[1] // 2 for h in halves)
    return pl.pallas_call(
        functools.partial(hidden_kernel, len(blocks), len(after)),
        out_shape=[
            jax.ShapeDtypeStruct((count, inner), jnp.bfloat16),
            jax.ShapeDtypeStruct((count, lane), jnp.float32),
        ],
        in_specs=[VMEM] * (len(blocks) + len(halves)) + [ANY] * len(after),
        out_specs=[VMEM, VMEM],
        scratch_shapes=[pltpu.VMEM((count, wide), jnp.bfloat16)],
        compiler_params=limit(6 if count <= 256 else 16),
        cost_estimate=pl.CostEstimate(flops=0, bytes_accessed=0, transcendentals=0),
        name="hidden",
    )(*blocks, *halves, *after)


def down_rows(hidden, share, down_ref, out_ref):
    count, width = out_ref.shape
    tile = min(256, count)
    step = 512
    for at in range(0, count, tile):
        for n in range(0, width, step):
            piece = jnp.dot(
                hidden[at : at + tile, :],
                down_ref[0, :, n : n + step],
                preferred_element_type=jnp.float32,
            )
            piece = piece.astype(jnp.bfloat16).astype(jnp.float32)
            terms = (share[at : at + tile, :1] * piece).astype(jnp.bfloat16)
            out_ref[at : at + tile, n : n + step] = terms


def away_kernel(sets, count, places, down_ref, *refs):
    hidden_refs, share_refs, refs = refs[:sets], refs[sets : 2 * sets], refs[2 * sets :]
    block_refs, gu_refs = refs[:count], refs[count:-7]
    away_ref, here_hidden, here_share, last_rows, last_hidden, last_share, hidden = refs[-7:]
    half = away_ref.shape[0]
    size = 2 * half // len(places)
    fill(last_rows, block_refs)
    hidden_and_share(last_rows, gu_refs, last_hidden, last_share)
    hidden_refs = (*hidden_refs, last_hidden)
    share_refs = (*share_refs, last_share)
    shares = []
    for to, (which, at) in enumerate(places):
        part = slice(at, at + size)
        place = slice(to * size % half, to * size % half + size)
        if to * size < half:
            hidden[place, :] = hidden_refs[which][part, :]
            shares.append(share_refs[which][part, :])
        else:
            here_hidden[place, :] = hidden_refs[which][part, :]
            here_share[place, :] = share_refs[which][part, :]
    down_rows(hidden, jnp.concatenate(shares, axis=0), down_ref, away_ref)


def here_kernel(down_ref, hidden_ref, share_ref, out_ref):
    down_rows(hidden_ref, share_ref, down_ref, out_ref)


def expert(down, hidden, shares, last, halves, places, rows):
    half = rows * len(places) // 2
    last_count = sum(b.shape[0] for b in last)
    _, inner, width = down.shape
    shape = jax.ShapeDtypeStruct
    away, here_hidden, here_share = pl.pallas_call(
        functools.partial(away_kernel, len(hidden), len(last), tuple(places)),
        out_shape=[
            shape((half, width), jnp.bfloat16),
            shape((half, inner), jnp.bfloat16),
            shape((half, lane), jnp.float32),
        ],
        in_specs=[VMEM] * (1 + 2 * len(hidden) + len(last) + len(halves)),
        out_specs=[VMEM] * 3,
        scratch_shapes=[
            pltpu.VMEM((last_count, width + lane), jnp.bfloat16),
            pltpu.VMEM((last_count, inner), jnp.bfloat16),
            pltpu.VMEM((last_count, lane), jnp.float32),
            pltpu.VMEM((half, inner), jnp.bfloat16),
        ],
        compiler_params=limit(8 if half <= 128 else 24),
        cost_estimate=pl.CostEstimate(
            flops=6 * half * width * inner, bytes_accessed=0, transcendentals=half * inner
        ),
        name="away",
    )(down, *hidden, *shares, *last, *halves)
    here = pl.pallas_call(
        here_kernel,
        out_shape=shape((half, width), jnp.bfloat16),
        in_specs=[VMEM] * 3,
        out_specs=VMEM,
        compiler_params=limit(4 if half <= 128 else 8),
        cost_estimate=pl.CostEstimate(
            flops=2 * half * width * inner, bytes_accessed=0, transcendentals=0
        ),
        name="here",
    )(down, here_hidden, here_share)
    return away, here


def add_kernel(pieces, got_ref, here_ref, *refs):
    later = (len(refs) - len(pieces)) // 2
    for piece, out_ref in zip(pieces, refs[later:]):
        to = 0
        for rows, columns in piece:
            here = here_ref[slice(*rows), slice(*columns)].astype(jnp.float32)
            got = got_ref[slice(*rows), slice(*columns)].astype(jnp.float32)
            end = to + columns[1] - columns[0]
            out_ref[:, to:end] = (got + here).astype(jnp.bfloat16)
            to = end
    for source, out_ref in zip(refs, refs[len(refs) - later :]):
        out_ref[...] = source[...]


def add(got, here, pieces, later=()):
    shapes = [(piece[0][0][1] - piece[0][0][0], sum(c[1] - c[0] for _, c in piece)) for piece in pieces]
    shapes += [array.shape for array in later]
    return pl.pallas_call(
        functools.partial(add_kernel, tuple(tuple(piece) for piece in pieces)),
        out_shape=[jax.ShapeDtypeStruct(shape, jnp.bfloat16) for shape in shapes],
        in_specs=[VMEM] * (2 + len(later)),
        out_specs=[VMEM] * len(shapes),
        compiler_params=limit(2 if got.shape[0] <= 16 else 6 if got.shape[0] <= 128 else 16),
        name="add",
    )(got, here, *later)


def swap(block, offset):
    count = lax.axis_size("ep")
    return lax.ppermute(block, "ep", [(i, i ^ offset) for i in range(count)])


def gather_blocks(block, far, gate_up):
    groups = gate_up.shape[3] // lane // 2
    lead, *late = far[:0:-1]
    close = far[0]
    along, beside = swap(block, lead), swap(block, 2)
    first, token = unpack(gate_up, 0, groups, [], 1 << 24)
    (again,) = join([[block]], [token])
    others = {offset: swap(again, offset) for offset in (*late, close, close ^ 2)}
    (early,) = join([[block, beside, along]], [])
    across = swap(along, 2)
    second, token = unpack(gate_up, groups, gate_up.shape[3] // lane - groups, [again], 1 << 24)
    halves = [first, second]
    middle, *held = join(
        [[across, *(others[o] for o in late)], *([others[o]] for o in late)], [token]
    )
    last = [swap(array, 2) for array in held]
    near = [early, middle, others[close], others[close ^ 2]]
    hidden, share = hidden_of(near, halves, [])
    *last, both = join([*([array] for array in last), near[2:]], [share])
    pairs = [swap(array, 1) for array in (*near[:2], both)]
    last = [*pairs, *last, *(swap(array, 1) for array in last)]
    keys = [0, 2, lead, lead ^ 2, *late, close, close ^ 2]
    ends = [o ^ 2 for o in late]
    keys = [keys, [*(o ^ 1 for o in keys), *ends, *(o ^ 1 for o in ends)]]
    return [hidden], [share], last, halves, keys


def shards(resid, norm_gain, expert_ids, route_weights, gate_up, down):
    owners = lax.axis_size("ep")
    tp = lax.axis_size("tp")
    far = tuple(range(4, owners, 4))
    resid_all = lax.all_gather(resid, "tp", axis=0, tiled=True) if tp > 1 else resid
    normed = norm(resid_all, norm_gain, expert_ids, route_weights)
    rows = normed.shape[0]
    hidden, shares, last, halves, keys = gather_blocks(normed, far, gate_up)
    order = sorted(range(owners), key=lambda o: (1 - (o & 1), 1 - (o >> 1 & 1), -o))
    found = {o: (which, at * rows) for which, part in enumerate(keys) for at, o in enumerate(part)}
    away, here = expert(down, hidden, shares, last, halves, [found[o] for o in order], rows)
    lead, *late = far[:0:-1]
    close = far[0]
    width = away.shape[1]
    cut = width // lane * 4 // 8 * lane
    keys = [o for o in order if o & 3 == 0]
    half = len(keys) * rows
    away_rows = {o: (at * rows, at * rows + rows) for at, o in enumerate(keys)}
    here_rows = {o: (half + at * rows, half + at * rows + rows) for at, o in enumerate(keys)}
    full, low, high = (0, width), (0, cut), (cut, width)
    pieces = {}
    for name, table in (("away", away_rows), ("here", here_rows)):
        pieces[name] = [(table[lead], full), *((table[o], low) for o in late)]
        pieces.update({(name, o): [(table[o], high)] for o in late})
        pieces.update({(name, o): [(table[o], full)] for o in (close, 0)})
    sums = dict(zip(pieces, add(swap(away, 1), here, list(pieces.values()))))
    got = swap(sums["away"], 2)
    direct = [swap(sums["here", o], o) for o in late]
    direct += [swap(sums["away", o], o ^ 2) for o in late]
    whole = [sums["here", 0], swap(sums["here", close], close)]
    whole.append(swap(sums["away", close], close ^ 2))
    later = [sums["away", 0]]
    ends = [width + at * cut for at in range(len(late) + 1)]
    parts = [full, *zip(ends, ends[1:])]
    total, *lows, own = add(got, sums["here"], [[((0, rows), part)] for part in parts], later)
    whole.append(swap(total, lead))
    summed = [swap(array, o) for o, array in zip(late, lows)]
    whole.append(swap(own, 2))
    mine = sum(array.astype(jnp.float32) for array in whole)
    halves = [sum(array.astype(jnp.float32) for array in part) for part in (summed, direct)]
    mine = mine + jnp.concatenate(halves, axis=1)
    if tp > 1:
        mine = lax.psum_scatter(mine, "tp", scatter_dimension=0, tiled=True)
    return (resid.astype(jnp.float32) + mine).astype(jnp.bfloat16)


def solution(mesh):
    return jax.shard_map(
        shards,
        mesh=mesh,
        in_specs=(
            P(("parts", "ep", "tp"), None),
            P(),
            P(("parts", "ep"), None),
            P(("parts", "ep"), None),
            P("ep", None, None, "tp"),
            P("ep", "tp", None),
        ),
        out_specs=P(("parts", "ep", "tp"), None),
        check_vma=False,
    )
```

```python
import functools

import jax
import jax.numpy as jnp
from jax import lax
from jax.experimental import pallas as pl
from jax.experimental.pallas import tpu as pltpu
from jax.sharding import PartitionSpec as P

eps = 1e-06
lane = 128
VMEM = pl.BlockSpec(memory_space=pltpu.VMEM)
ANY = pl.BlockSpec(memory_space=pl.ANY)
HBM = pl.BlockSpec(memory_space=pltpu.HBM)


def limit(mib):
    return pltpu.CompilerParams(vmem_limit_bytes=mib << 20)


def in_hbm(array):
    return pltpu.with_memory_space_constraint(array, pltpu.HBM)


def in_vmem(array):
    return pltpu.with_memory_space_constraint(array, pltpu.VMEM)


def norm_kernel(*refs):
    sources, out_ref, held, sems = refs[:4], refs[4], refs[5:9], refs[9]
    copies = [
        pltpu.make_async_copy(source, ref, sems.at[i])
        for i, (source, ref) in enumerate(zip(sources, held))
    ]
    for copy in copies:
        copy.start()
    for copy in copies:
        copy.wait()
    resid_ref, gain_ref, ids_ref, weights_ref = held
    rows, width = resid_ref.shape
    values = resid_ref[...].astype(jnp.float32)
    scale = lax.rsqrt(jnp.mean(values * values, axis=-1, keepdims=True) + eps)
    gain = gain_ref[...].reshape(1, width)
    out_ref[:, :width] = (values * scale * gain).astype(jnp.bfloat16)
    chosen, count = ids_ref.shape
    experts = lax.broadcasted_iota(jnp.int32, (lane, count), 0)
    share = jnp.zeros((lane, count), jnp.float32)
    for k in range(chosen):
        weight = weights_ref[k : k + 1, :].astype(jnp.float32)
        share = share + jnp.where(experts == ids_ref[k : k + 1, :], weight, 0.0)
    out_ref[:, width:] = share.T.astype(jnp.bfloat16)


def norm(resid, gain, ids, weights):
    rows, width = resid.shape
    sources = [resid, gain, ids.T, weights.T]
    return pl.pallas_call(
        norm_kernel,
        out_shape=jax.ShapeDtypeStruct((rows, width + lane), jnp.bfloat16),
        in_specs=[HBM] * 4,
        out_specs=VMEM,
        scratch_shapes=[pltpu.VMEM(a.shape, a.dtype) for a in sources]
        + [pltpu.SemaphoreType.DMA((4,))],
        compiler_params=limit(3),
        name="norm",
    )(*[in_hbm(a) for a in sources])


def unpack_kernel(first, packed_ref, *refs):
    out_ref, token_ref, buffer, sems = refs[-4:]
    token_ref[...] = jnp.zeros_like(token_ref)
    width = packed_ref.shape[1]
    groups = buffer.shape[0]
    inner = groups * lane
    cuts = sems.shape[1]
    depth = width // cuts
    copies = {
        (c, part): pltpu.make_async_copy(
            packed_ref.at[
                0,
                part * depth : (part + 1) * depth,
                :,
                (first + c) * lane : (first + c + 1) * lane,
            ],
            buffer.at[c, part * depth : (part + 1) * depth],
            sems.at[c, part],
        )
        for c in range(groups)
        for part in range(cuts)
    }
    for copy in copies.values():
        copy.start()
    tile = 128
    for (c, part), copy in copies.items():
        copy.wait()
        rows = buffer.at[c].reshape(2 * width, lane)

        def step(i, _):
            at = part * depth + i * tile
            both = rows.at[pl.ds(pl.multiple_of(2 * at, 2 * tile), 2 * tile), :]
            to = pl.ds(pl.multiple_of(at, tile), tile)
            out_ref[to, c * lane : (c + 1) * lane] = both[pl.ds(0, tile, stride=2), :]
            out_ref[to, inner + c * lane : inner + (c + 1) * lane] = both[
                pl.ds(1, tile, stride=2), :
            ]
            return 0

        lax.fori_loop(0, depth // tile, step, 0, unroll=7)


def unpack(packed, first, groups, after, cost=0):
    width = packed.shape[1]
    return pl.pallas_call(
        functools.partial(unpack_kernel, first),
        out_shape=[
            jax.ShapeDtypeStruct((width, 2 * groups * lane), jnp.bfloat16),
            jax.ShapeDtypeStruct((8, lane), jnp.float32),
        ],
        in_specs=[HBM] + [ANY] * len(after),
        out_specs=[VMEM, VMEM],
        scratch_shapes=[
            pltpu.VMEM((groups, width, 2, lane), jnp.bfloat16),
            pltpu.SemaphoreType.DMA((groups, 4)),
        ],
        compiler_params=limit(9),
        cost_estimate=pl.CostEstimate(flops=0, bytes_accessed=cost, transcendentals=0),
        name="unpack",
    )(in_hbm(packed), *after)


def join_kernel(sizes, *refs):
    sources, out_refs = refs[: sum(sizes)], refs[-len(sizes) :]
    at = 0
    for size, out_ref in zip(sizes, out_refs):
        to = 0
        for source in sources[at : at + size]:
            rows = source.shape[0]
            out_ref[to : to + rows, :] = source[...]
            to += rows
        at += size


def join(groups, after):
    blocks = [block for group in groups for block in group]
    shapes = [(sum(b.shape[0] for b in group), group[0].shape[1]) for group in groups]
    return pl.pallas_call(
        functools.partial(join_kernel, tuple(len(group) for group in groups)),
        out_shape=[jax.ShapeDtypeStruct(shape, jnp.bfloat16) for shape in shapes],
        in_specs=[VMEM] * len(blocks) + [ANY] * len(after),
        out_specs=[VMEM] * len(groups),
        compiler_params=limit(4 if len(blocks) < 8 else 12),
        name="join",
    )(*blocks, *after)


def hidden_rows(rows_ref, gu_refs, hidden, at, tile):
    to = 0
    rows = rows_ref[at : at + tile, : gu_refs[0].shape[0]]
    for gu_ref in gu_refs:
        half = gu_ref.shape[1] // 2
        step = min(256, half)
        for n in range(0, half, step):
            gate = jnp.dot(rows, gu_ref[:, n : n + step], preferred_element_type=jnp.float32)
            up = jnp.dot(
                rows, gu_ref[:, half + n : half + n + step], preferred_element_type=jnp.float32
            )
            hidden[at : at + tile, to : to + step] = (jax.nn.silu(gate) * up).astype(jnp.bfloat16)
            to += step


def fill(rows_ref, block_refs):
    to = 0
    for block_ref in block_refs:
        rows = block_ref.shape[0]
        rows_ref[to : to + rows, :] = block_ref[...]
        to += rows


def hidden_and_share(rows_ref, gu_refs, hidden, share_ref):
    rows = rows_ref.shape[0]
    width = gu_refs[0].shape[0]
    tile = min(256, rows)
    for at in range(0, rows, tile):
        hidden_rows(rows_ref, gu_refs, hidden, at, min(tile, rows - at))
    shares = rows_ref[:, width:].astype(jnp.float32)
    lanes = lax.broadcasted_iota(jnp.int32, shares.shape, 1)
    mine = jnp.where(lanes == lax.axis_index("ep"), shares, 0.0)
    share_ref[...] = jnp.broadcast_to(jnp.sum(mine, axis=1, keepdims=True), shares.shape)


def hidden_kernel(count, after, *refs):
    block_refs, gu_refs = refs[:count], refs[count : -3 - after]
    hidden, share_ref, rows_ref = refs[-3:]
    fill(rows_ref, block_refs)
    hidden_and_share(rows_ref, gu_refs, hidden, share_ref)


def hidden_of(blocks, halves, after):
    count, wide = sum(b.shape[0] for b in blocks), blocks[0].shape[1]
    width, inner = halves[0].shape[0], sum(h.shape[1] // 2 for h in halves)
    return pl.pallas_call(
        functools.partial(hidden_kernel, len(blocks), len(after)),
        out_shape=[
            jax.ShapeDtypeStruct((count, inner), jnp.bfloat16),
            jax.ShapeDtypeStruct((count, lane), jnp.float32),
        ],
        in_specs=[VMEM] * (len(blocks) + len(halves)) + [ANY] * len(after),
        out_specs=[VMEM, VMEM],
        scratch_shapes=[pltpu.VMEM((count, wide), jnp.bfloat16)],
        compiler_params=limit(6 if count <= 256 else 16),
        cost_estimate=pl.CostEstimate(flops=0, bytes_accessed=0, transcendentals=0),
        name="hidden",
    )(*blocks, *halves, *after)


def down_rows(hidden, share, down_ref, out_ref):
    count, width = out_ref.shape
    tile = min(256, count)
    step = 512
    for at in range(0, count, tile):
        for n in range(0, width, step):
            piece = jnp.dot(
                hidden[at : at + tile, :],
                down_ref[0, :, n : n + step],
                preferred_element_type=jnp.float32,
            )
            piece = piece.astype(jnp.bfloat16).astype(jnp.float32)
            terms = (share[at : at + tile, :1] * piece).astype(jnp.bfloat16)
            out_ref[at : at + tile, n : n + step] = terms


def away_kernel(sets, count, places, down_ref, *refs):
    hidden_refs, share_refs, refs = refs[:sets], refs[sets : 2 * sets], refs[2 * sets :]
    block_refs, gu_refs = refs[:count], refs[count:-7]
    away_ref, here_hidden, here_share, last_rows, last_hidden, last_share, hidden = refs[-7:]
    half = away_ref.shape[0]
    size = 2 * half // len(places)
    fill(last_rows, block_refs)
    hidden_and_share(last_rows, gu_refs, last_hidden, last_share)
    hidden_refs = (*hidden_refs, last_hidden)
    share_refs = (*share_refs, last_share)
    shares = []
    for to, (which, at) in enumerate(places):
        part = slice(at, at + size)
        place = slice(to * size % half, to * size % half + size)
        if to * size < half:
            hidden[place, :] = hidden_refs[which][part, :]
            shares.append(share_refs[which][part, :])
        else:
            here_hidden[place, :] = hidden_refs[which][part, :]
            here_share[place, :] = share_refs[which][part, :]
    down_rows(hidden, jnp.concatenate(shares, axis=0), down_ref, away_ref)


def here_kernel(down_ref, hidden_ref, share_ref, out_ref):
    down_rows(hidden_ref, share_ref, down_ref, out_ref)


def expert(down, hidden, shares, last, halves, places, rows):
    half = rows * len(places) // 2
    last_count = sum(b.shape[0] for b in last)
    _, inner, width = down.shape
    shape = jax.ShapeDtypeStruct
    away, here_hidden, here_share = pl.pallas_call(
        functools.partial(away_kernel, len(hidden), len(last), tuple(places)),
        out_shape=[
            shape((half, width), jnp.bfloat16),
            shape((half, inner), jnp.bfloat16),
            shape((half, lane), jnp.float32),
        ],
        in_specs=[VMEM] * (1 + 2 * len(hidden) + len(last) + len(halves)),
        out_specs=[VMEM] * 3,
        scratch_shapes=[
            pltpu.VMEM((last_count, width + lane), jnp.bfloat16),
            pltpu.VMEM((last_count, inner), jnp.bfloat16),
            pltpu.VMEM((last_count, lane), jnp.float32),
            pltpu.VMEM((half, inner), jnp.bfloat16),
        ],
        compiler_params=limit(8 if half <= 128 else 24),
        cost_estimate=pl.CostEstimate(
            flops=6 * half * width * inner, bytes_accessed=0, transcendentals=half * inner
        ),
        name="away",
    )(down, *hidden, *shares, *last, *halves)
    here = pl.pallas_call(
        here_kernel,
        out_shape=shape((half, width), jnp.bfloat16),
        in_specs=[VMEM] * 3,
        out_specs=VMEM,
        compiler_params=limit(4 if half <= 128 else 8),
        cost_estimate=pl.CostEstimate(
            flops=2 * half * width * inner, bytes_accessed=0, transcendentals=0
        ),
        name="here",
    )(down, here_hidden, here_share)
    return away, here


def add_kernel(pieces, got_ref, here_ref, *refs):
    later = (len(refs) - len(pieces)) // 2
    for piece, out_ref in zip(pieces, refs[later:]):
        to = 0
        for rows, columns in piece:
            here = here_ref[slice(*rows), slice(*columns)].astype(jnp.float32)
            got = got_ref[slice(*rows), slice(*columns)].astype(jnp.float32)
            end = to + columns[1] - columns[0]
            out_ref[:, to:end] = (got + here).astype(jnp.bfloat16)
            to = end
    for source, out_ref in zip(refs, refs[len(refs) - later :]):
        out_ref[...] = source[...]


def add(got, here, pieces, later=()):
    shapes = [(piece[0][0][1] - piece[0][0][0], sum(c[1] - c[0] for _, c in piece)) for piece in pieces]
    shapes += [array.shape for array in later]
    return pl.pallas_call(
        functools.partial(add_kernel, tuple(tuple(piece) for piece in pieces)),
        out_shape=[jax.ShapeDtypeStruct(shape, jnp.bfloat16) for shape in shapes],
        in_specs=[VMEM] * (2 + len(later)),
        out_specs=[VMEM] * len(shapes),
        compiler_params=limit(2 if got.shape[0] <= 16 else 6 if got.shape[0] <= 128 else 16),
        name="add",
    )(got, here, *later)


def swap(block, offset):
    count = lax.axis_size("ep")
    return lax.ppermute(block, "ep", [(i, i ^ offset) for i in range(count)])


def gather_blocks(block, far, gate_up):
    groups = gate_up.shape[3] // lane // 2
    lead, *late = far[:0:-1]
    close = far[0]
    along, beside = swap(block, lead), swap(block, 2)
    first, token = unpack(gate_up, 0, groups, [], 1 << 24)
    (again,) = join([[block]], [token])
    others = {offset: swap(again, offset) for offset in (*late, close, close ^ 2)}
    (early,) = join([[block, beside, along]], [])
    across = swap(along, 2)
    second, token = unpack(gate_up, groups, gate_up.shape[3] // lane - groups, [again], 1 << 24)
    halves = [first, second]
    middle, *held = join(
        [[across, *(others[o] for o in late)], *([others[o]] for o in late)], [token]
    )
    last = [swap(array, 2) for array in held]
    near = [early, middle, others[close], others[close ^ 2]]
    hidden, share = hidden_of(near, halves, [])
    *last, both = join([*([array] for array in last), near[2:]], [share])
    pairs = [swap(array, 1) for array in (*near[:2], both)]
    last = [*pairs, *last, *(swap(array, 1) for array in last)]
    keys = [0, 2, lead, lead ^ 2, *late, close, close ^ 2]
    ends = [o ^ 2 for o in late]
    keys = [keys, [*(o ^ 1 for o in keys), *ends, *(o ^ 1 for o in ends)]]
    return [hidden], [share], last, halves, keys


def shards(resid, norm_gain, expert_ids, route_weights, gate_up, down):
    owners = lax.axis_size("ep")
    tp = lax.axis_size("tp")
    far = tuple(range(4, owners, 4))
    resid_all = lax.all_gather(resid, "tp", axis=0, tiled=True) if tp > 1 else resid
    normed = norm(resid_all, norm_gain, expert_ids, route_weights)
    rows = normed.shape[0]
    hidden, shares, last, halves, keys = gather_blocks(normed, far, gate_up)
    order = sorted(range(owners), key=lambda o: (1 - (o & 1), 1 - (o >> 1 & 1), -o))
    found = {o: (which, at * rows) for which, part in enumerate(keys) for at, o in enumerate(part)}
    away, here = expert(down, hidden, shares, last, halves, [found[o] for o in order], rows)
    lead, *late = far[:0:-1]
    close = far[0]
    width = away.shape[1]
    cut = width // lane * 4 // 8 * lane
    keys = [o for o in order if o & 3 == 0]
    half = len(keys) * rows
    away_rows = {o: (at * rows, at * rows + rows) for at, o in enumerate(keys)}
    here_rows = {o: (half + at * rows, half + at * rows + rows) for at, o in enumerate(keys)}
    full, low, high = (0, width), (0, cut), (cut, width)
    pieces = {}
    for name, table in (("away", away_rows), ("here", here_rows)):
        pieces[name] = [(table[lead], full), *((table[o], low) for o in late)]
        pieces.update({(name, o): [(table[o], high)] for o in late})
        pieces.update({(name, o): [(table[o], full)] for o in (close, 0)})
    sums = dict(zip(pieces, add(swap(away, 1), here, list(pieces.values()))))
    got = swap(sums["away"], 2)
    direct = [swap(sums["here", o], o) for o in late]
    direct += [swap(sums["away", o], o ^ 2) for o in late]
    whole = [sums["here", 0], swap(sums["here", close], close)]
    whole.append(swap(sums["away", close], close ^ 2))
    own = sums["away", 0]
    later = []
    ends = [width + at * cut for at in range(len(late) + 1)]
    parts = [full, *zip(ends, ends[1:])]
    total, *lows = add(got, sums["here"], [[((0, rows), part)] for part in parts], later)
    whole.append(swap(total, lead))
    summed = [swap(array, o) for o, array in zip(late, lows)]
    whole.append(swap(own, 2))
    mine = sum(array.astype(jnp.float32) for array in whole)
    halves = [sum(array.astype(jnp.float32) for array in part) for part in (summed, direct)]
    mine = mine + jnp.concatenate(halves, axis=1)
    if tp > 1:
        mine = lax.psum_scatter(mine, "tp", scatter_dimension=0, tiled=True)
    return (resid.astype(jnp.float32) + mine).astype(jnp.bfloat16)


def solution(mesh):
    return jax.shard_map(
        shards,
        mesh=mesh,
        in_specs=(
            P(("parts", "ep", "tp"), None),
            P(),
            P(("parts", "ep"), None),
            P(("parts", "ep"), None),
            P("ep", None, None, "tp"),
            P("ep", "tp", None),
        ),
        out_specs=P(("parts", "ep", "tp"), None),
        check_vma=False,
    )
```

```python
import functools

import jax
import jax.numpy as jnp
from jax import lax
from jax.experimental import pallas as pl
from jax.experimental.pallas import tpu as pltpu
from jax.sharding import PartitionSpec as P

eps = 1e-06
lane = 128
VMEM = pl.BlockSpec(memory_space=pltpu.VMEM)
ANY = pl.BlockSpec(memory_space=pl.ANY)
HBM = pl.BlockSpec(memory_space=pltpu.HBM)


def limit(mib):
    return pltpu.CompilerParams(vmem_limit_bytes=mib << 20)


def in_hbm(array):
    return pltpu.with_memory_space_constraint(array, pltpu.HBM)


def in_vmem(array):
    return pltpu.with_memory_space_constraint(array, pltpu.VMEM)


def norm_kernel(*refs):
    sources, out_ref, held, sems = refs[:4], refs[4], refs[5:9], refs[9]
    copies = [
        pltpu.make_async_copy(source, ref, sems.at[i])
        for i, (source, ref) in enumerate(zip(sources, held))
    ]
    for copy in copies:
        copy.start()
    for copy in copies:
        copy.wait()
    resid_ref, gain_ref, ids_ref, weights_ref = held
    rows, width = resid_ref.shape
    values = resid_ref[...].astype(jnp.float32)
    scale = lax.rsqrt(jnp.mean(values * values, axis=-1, keepdims=True) + eps)
    gain = gain_ref[...].reshape(1, width)
    out_ref[:, :width] = (values * scale * gain).astype(jnp.bfloat16)
    chosen, count = ids_ref.shape
    experts = lax.broadcasted_iota(jnp.int32, (lane, count), 0)
    share = jnp.zeros((lane, count), jnp.float32)
    for k in range(chosen):
        weight = weights_ref[k : k + 1, :].astype(jnp.float32)
        share = share + jnp.where(experts == ids_ref[k : k + 1, :], weight, 0.0)
    out_ref[:, width:] = share.T.astype(jnp.bfloat16)


def norm(resid, gain, ids, weights):
    rows, width = resid.shape
    sources = [resid, gain, ids.T, weights.T]
    return pl.pallas_call(
        norm_kernel,
        out_shape=jax.ShapeDtypeStruct((rows, width + lane), jnp.bfloat16),
        in_specs=[HBM] * 4,
        out_specs=VMEM,
        scratch_shapes=[pltpu.VMEM(a.shape, a.dtype) for a in sources]
        + [pltpu.SemaphoreType.DMA((4,))],
        compiler_params=limit(3),
        name="norm",
    )(*[in_hbm(a) for a in sources])


def unpack_kernel(first, packed_ref, *refs):
    out_ref, token_ref, buffer, sems = refs[-4:]
    token_ref[...] = jnp.zeros_like(token_ref)
    width = packed_ref.shape[1]
    groups = buffer.shape[0]
    inner = groups * lane
    cuts = sems.shape[1]
    depth = width // cuts
    copies = {
        (c, part): pltpu.make_async_copy(
            packed_ref.at[
                0,
                part * depth : (part + 1) * depth,
                :,
                (first + c) * lane : (first + c + 1) * lane,
            ],
            buffer.at[c, part * depth : (part + 1) * depth],
            sems.at[c, part],
        )
        for c in range(groups)
        for part in range(cuts)
    }
    for copy in copies.values():
        copy.start()
    tile = 128
    for (c, part), copy in copies.items():
        copy.wait()
        rows = buffer.at[c].reshape(2 * width, lane)

        def step(i, _):
            at = part * depth + i * tile
            both = rows.at[pl.ds(pl.multiple_of(2 * at, 2 * tile), 2 * tile), :]
            to = pl.ds(pl.multiple_of(at, tile), tile)
            out_ref[to, c * lane : (c + 1) * lane] = both[pl.ds(0, tile, stride=2), :]
            out_ref[to, inner + c * lane : inner + (c + 1) * lane] = both[
                pl.ds(1, tile, stride=2), :
            ]
            return 0

        lax.fori_loop(0, depth // tile, step, 0, unroll=7)


def unpack(packed, first, groups, after, cost=0):
    width = packed.shape[1]
    return pl.pallas_call(
        functools.partial(unpack_kernel, first),
        out_shape=[
            jax.ShapeDtypeStruct((width, 2 * groups * lane), jnp.bfloat16),
            jax.ShapeDtypeStruct((8, lane), jnp.float32),
        ],
        in_specs=[HBM] + [ANY] * len(after),
        out_specs=[VMEM, VMEM],
        scratch_shapes=[
            pltpu.VMEM((groups, width, 2, lane), jnp.bfloat16),
            pltpu.SemaphoreType.DMA((groups, 4)),
        ],
        compiler_params=limit(9),
        cost_estimate=pl.CostEstimate(flops=0, bytes_accessed=cost, transcendentals=0),
        name="unpack",
    )(in_hbm(packed), *after)


def join_kernel(sizes, *refs):
    sources, out_refs = refs[: sum(sizes)], refs[-len(sizes) :]
    at = 0
    for size, out_ref in zip(sizes, out_refs):
        to = 0
        for source in sources[at : at + size]:
            rows = source.shape[0]
            out_ref[to : to + rows, :] = source[...]
            to += rows
        at += size


def join(groups, after):
    blocks = [block for group in groups for block in group]
    shapes = [(sum(b.shape[0] for b in group), group[0].shape[1]) for group in groups]
    return pl.pallas_call(
        functools.partial(join_kernel, tuple(len(group) for group in groups)),
        out_shape=[jax.ShapeDtypeStruct(shape, jnp.bfloat16) for shape in shapes],
        in_specs=[VMEM] * len(blocks) + [ANY] * len(after),
        out_specs=[VMEM] * len(groups),
        compiler_params=limit(4 if len(blocks) < 8 else 12),
        name="join",
    )(*blocks, *after)


def hidden_rows(rows_ref, gu_refs, hidden, at, tile):
    to = 0
    rows = rows_ref[at : at + tile, : gu_refs[0].shape[0]]
    for gu_ref in gu_refs:
        half = gu_ref.shape[1] // 2
        step = min(256, half)
        for n in range(0, half, step):
            gate = jnp.dot(rows, gu_ref[:, n : n + step], preferred_element_type=jnp.float32)
            up = jnp.dot(
                rows, gu_ref[:, half + n : half + n + step], preferred_element_type=jnp.float32
            )
            hidden[at : at + tile, to : to + step] = (jax.nn.silu(gate) * up).astype(jnp.bfloat16)
            to += step


def fill(rows_ref, block_refs):
    to = 0
    for block_ref in block_refs:
        rows = block_ref.shape[0]
        rows_ref[to : to + rows, :] = block_ref[...]
        to += rows


def hidden_and_share(rows_ref, gu_refs, hidden, share_ref):
    rows = rows_ref.shape[0]
    width = gu_refs[0].shape[0]
    tile = min(256, rows)
    for at in range(0, rows, tile):
        hidden_rows(rows_ref, gu_refs, hidden, at, min(tile, rows - at))
    shares = rows_ref[:, width:].astype(jnp.float32)
    lanes = lax.broadcasted_iota(jnp.int32, shares.shape, 1)
    mine = jnp.where(lanes == lax.axis_index("ep"), shares, 0.0)
    share_ref[...] = jnp.broadcast_to(jnp.sum(mine, axis=1, keepdims=True), shares.shape)


def hidden_kernel(count, after, *refs):
    block_refs, gu_refs = refs[:count], refs[count : -3 - after]
    hidden, share_ref, rows_ref = refs[-3:]
    used = sum(ref.shape[0] for ref in block_refs)
    fill(rows_ref, block_refs)
    rows_ref[used:, :] = jnp.zeros_like(rows_ref[used:, :])
    hidden_and_share(rows_ref, gu_refs, hidden, share_ref)


def hidden_of(blocks, halves, after):
    count, wide = sum(b.shape[0] for b in blocks), blocks[0].shape[1]
    count += -count % lane
    width, inner = halves[0].shape[0], sum(h.shape[1] // 2 for h in halves)
    return pl.pallas_call(
        functools.partial(hidden_kernel, len(blocks), len(after)),
        out_shape=[
            jax.ShapeDtypeStruct((count, inner), jnp.bfloat16),
            jax.ShapeDtypeStruct((count, lane), jnp.float32),
        ],
        in_specs=[VMEM] * (len(blocks) + len(halves)) + [ANY] * len(after),
        out_specs=[VMEM, VMEM],
        scratch_shapes=[pltpu.VMEM((count, wide), jnp.bfloat16)],
        compiler_params=limit(6 if count <= 256 else 16),
        cost_estimate=pl.CostEstimate(flops=0, bytes_accessed=0, transcendentals=0),
        name="hidden",
    )(*blocks, *halves, *after)


def down_rows(hidden, share, down_ref, out_ref):
    count, width = out_ref.shape
    tile = min(256, count)
    step = 512
    for at in range(0, count, tile):
        for n in range(0, width, step):
            piece = jnp.dot(
                hidden[at : at + tile, :],
                down_ref[0, :, n : n + step],
                preferred_element_type=jnp.float32,
            )
            piece = piece.astype(jnp.bfloat16).astype(jnp.float32)
            terms = (share[at : at + tile, :1] * piece).astype(jnp.bfloat16)
            out_ref[at : at + tile, n : n + step] = terms


def away_kernel(sets, count, places, down_ref, *refs):
    hidden_refs, share_refs, refs = refs[:sets], refs[sets : 2 * sets], refs[2 * sets :]
    block_refs, gu_refs = refs[:count], refs[count:-7]
    away_ref, here_hidden, here_share, last_rows, last_hidden, last_share, hidden = refs[-7:]
    half = away_ref.shape[0]
    size = 2 * half // len(places)
    fill(last_rows, block_refs)
    hidden_and_share(last_rows, gu_refs, last_hidden, last_share)
    hidden_refs = (*hidden_refs, last_hidden)
    share_refs = (*share_refs, last_share)
    shares = []
    for to, (which, at) in enumerate(places):
        part = slice(at, at + size)
        place = slice(to * size % half, to * size % half + size)
        if to * size < half:
            hidden[place, :] = hidden_refs[which][part, :]
            shares.append(share_refs[which][part, :])
        else:
            here_hidden[place, :] = hidden_refs[which][part, :]
            here_share[place, :] = share_refs[which][part, :]
    down_rows(hidden, jnp.concatenate(shares, axis=0), down_ref, away_ref)


def here_kernel(down_ref, hidden_ref, share_ref, out_ref):
    down_rows(hidden_ref, share_ref, down_ref, out_ref)


def expert(down, hidden, shares, last, halves, places, rows):
    half = rows * len(places) // 2
    last_count = sum(b.shape[0] for b in last)
    _, inner, width = down.shape
    shape = jax.ShapeDtypeStruct
    away, here_hidden, here_share = pl.pallas_call(
        functools.partial(away_kernel, len(hidden), len(last), tuple(places)),
        out_shape=[
            shape((half, width), jnp.bfloat16),
            shape((half, inner), jnp.bfloat16),
            shape((half, lane), jnp.float32),
        ],
        in_specs=[VMEM] * (1 + 2 * len(hidden) + len(last) + len(halves)),
        out_specs=[VMEM] * 3,
        scratch_shapes=[
            pltpu.VMEM((last_count, width + lane), jnp.bfloat16),
            pltpu.VMEM((last_count, inner), jnp.bfloat16),
            pltpu.VMEM((last_count, lane), jnp.float32),
            pltpu.VMEM((half, inner), jnp.bfloat16),
        ],
        compiler_params=limit(8 if half <= 128 else 24),
        cost_estimate=pl.CostEstimate(
            flops=6 * half * width * inner, bytes_accessed=0, transcendentals=half * inner
        ),
        name="away",
    )(down, *hidden, *shares, *last, *halves)
    here = pl.pallas_call(
        here_kernel,
        out_shape=shape((half, width), jnp.bfloat16),
        in_specs=[VMEM] * 3,
        out_specs=VMEM,
        compiler_params=limit(4 if half <= 128 else 8),
        cost_estimate=pl.CostEstimate(
            flops=2 * half * width * inner, bytes_accessed=0, transcendentals=0
        ),
        name="here",
    )(down, here_hidden, here_share)
    return away, here


def add_kernel(pieces, got_ref, here_ref, *refs):
    later = (len(refs) - len(pieces)) // 2
    for piece, out_ref in zip(pieces, refs[later:]):
        to = 0
        for rows, columns in piece:
            here = here_ref[slice(*rows), slice(*columns)].astype(jnp.float32)
            got = got_ref[slice(*rows), slice(*columns)].astype(jnp.float32)
            end = to + columns[1] - columns[0]
            out_ref[:, to:end] = (got + here).astype(jnp.bfloat16)
            to = end
    for source, out_ref in zip(refs, refs[len(refs) - later :]):
        out_ref[...] = source[...]


def add(got, here, pieces, later=()):
    shapes = [(piece[0][0][1] - piece[0][0][0], sum(c[1] - c[0] for _, c in piece)) for piece in pieces]
    shapes += [array.shape for array in later]
    return pl.pallas_call(
        functools.partial(add_kernel, tuple(tuple(piece) for piece in pieces)),
        out_shape=[jax.ShapeDtypeStruct(shape, jnp.bfloat16) for shape in shapes],
        in_specs=[VMEM] * (2 + len(later)),
        out_specs=[VMEM] * len(shapes),
        compiler_params=limit(2 if got.shape[0] <= 16 else 6 if got.shape[0] <= 128 else 16),
        name="add",
    )(got, here, *later)


def swap(block, offset):
    count = lax.axis_size("ep")
    return lax.ppermute(block, "ep", [(i, i ^ offset) for i in range(count)])


def gather_blocks(block, far, gate_up):
    groups = gate_up.shape[3] // lane // 2
    lead, *late = far[:0:-1]
    close = far[0]
    along, beside = swap(block, lead), swap(block, 2)
    first, token = unpack(gate_up, 0, groups, [], 1 << 24)
    (again,) = join([[block]], [token])
    others = {offset: swap(again, offset) for offset in (*late, close, close ^ 2)}
    (early,) = join([[block, beside, along]], [])
    across = swap(along, 2)
    second, token = unpack(gate_up, groups, gate_up.shape[3] // lane - groups, [again], 1 << 24)
    halves = [first, second]
    middle, *held = join(
        [[across, *(others[o] for o in late)], *([others[o]] for o in late)], [token]
    )
    last = [swap(array, 2) for array in held]
    near = [early, middle, others[close], others[close ^ 2]]
    hidden, share = hidden_of(near, halves, [])
    *last, both = join([*([array] for array in last), near[2:]], [share])
    pairs = [swap(array, 1) for array in (*near[:2], both)]
    last = [*pairs, *last, *(swap(array, 1) for array in last)]
    keys = [0, 2, lead, lead ^ 2, *late, close, close ^ 2]
    ends = [o ^ 2 for o in late]
    keys = [keys, [*(o ^ 1 for o in keys), *ends, *(o ^ 1 for o in ends)]]
    return [hidden], [share], last, halves, keys


def shards(resid, norm_gain, expert_ids, route_weights, gate_up, down):
    owners = lax.axis_size("ep")
    tp = lax.axis_size("tp")
    far = tuple(range(4, owners, 4))
    resid_all = lax.all_gather(resid, "tp", axis=0, tiled=True) if tp > 1 else resid
    normed = norm(resid_all, norm_gain, expert_ids, route_weights)
    rows = normed.shape[0]
    hidden, shares, last, halves, keys = gather_blocks(normed, far, gate_up)
    order = sorted(range(owners), key=lambda o: (1 - (o & 1), 1 - (o >> 1 & 1), -o))
    found = {o: (which, at * rows) for which, part in enumerate(keys) for at, o in enumerate(part)}
    away, here = expert(down, hidden, shares, last, halves, [found[o] for o in order], rows)
    lead, *late = far[:0:-1]
    close = far[0]
    width = away.shape[1]
    cut = width // lane * 4 // 8 * lane
    keys = [o for o in order if o & 3 == 0]
    half = len(keys) * rows
    away_rows = {o: (at * rows, at * rows + rows) for at, o in enumerate(keys)}
    here_rows = {o: (half + at * rows, half + at * rows + rows) for at, o in enumerate(keys)}
    full, low, high = (0, width), (0, cut), (cut, width)
    pieces = {}
    for name, table in (("away", away_rows), ("here", here_rows)):
        pieces[name] = [(table[lead], full), *((table[o], low) for o in late)]
        pieces.update({(name, o): [(table[o], high)] for o in late})
        pieces.update({(name, o): [(table[o], full)] for o in (close, 0)})
    sums = dict(zip(pieces, add(swap(away, 1), here, list(pieces.values()))))
    got = swap(sums["away"], 2)
    direct = [swap(sums["here", o], o) for o in late]
    direct += [swap(sums["away", o], o ^ 2) for o in late]
    whole = [sums["here", 0], swap(sums["here", close], close)]
    whole.append(swap(sums["away", close], close ^ 2))
    own = sums["away", 0]
    later = []
    ends = [width + at * cut for at in range(len(late) + 1)]
    parts = [full, *zip(ends, ends[1:])]
    total, *lows = add(got, sums["here"], [[((0, rows), part)] for part in parts], later)
    whole.append(swap(total, lead))
    summed = [swap(array, o) for o, array in zip(late, lows)]
    whole.append(swap(own, 2))
    mine = sum(array.astype(jnp.float32) for array in whole)
    halves = [sum(array.astype(jnp.float32) for array in part) for part in (summed, direct)]
    mine = mine + jnp.concatenate(halves, axis=1)
    if tp > 1:
        mine = lax.psum_scatter(mine, "tp", scatter_dimension=0, tiled=True)
    return (resid.astype(jnp.float32) + mine).astype(jnp.bfloat16)


def solution(mesh):
    return jax.shard_map(
        shards,
        mesh=mesh,
        in_specs=(
            P(("parts", "ep", "tp"), None),
            P(),
            P(("parts", "ep"), None),
            P(("parts", "ep"), None),
            P("ep", None, None, "tp"),
            P("ep", "tp", None),
        ),
        out_specs=P(("parts", "ep", "tp"), None),
        check_vma=False,
    )
```
